128 devices in a mesh: expert: 16 (over y, x_hi, core), tensor: 8 (over z, x_lo).
Axes of the slice: x: 4 (x_hi: 2, x_lo: 2; x = x_hi * 2 + x_lo), y: 4, z: 4, core: 2. Of those that a mesh axis runs over, the one named last changes fastest.
Arguments:
- tokens: bfloat16 [2048, 4096], P('expert', 'tensor'), may hold values from -6 to 6
- gates: float32 [2048, 2], P('expert'), may hold values from 0.1 to 0.9
- expert_ids: int32 [2048, 2], P('expert'), may hold values from 0 to 3, all different within a row; in each aligned block of 128 rows (0 to 127, 128 to 255, ...) at most 68 rows name the same one
- w_in: bfloat16 [16, 4096, 4096], P('expert', None, 'tensor'), may hold values from -0.09375 to 0.09375
- w_out: bfloat16 [16, 4096, 4096], P('expert', 'tensor'), may hold values from -0.046875 to 0.046875
- out_grad: bfloat16 [2048, 4096], P('expert', 'tensor'), may hold values from -6 to 6
Outputs:
- combined: bfloat16 [2048, 4096], P('expert', 'tensor')
- token_grad: bfloat16 [2048, 4096], P('expert', 'tensor')
- gate_grad: float32 [2048, 2], P('expert')
- w_in_grad: bfloat16 [16, 4096, 4096], P('expert', None, 'tensor')
- w_out_grad: bfloat16 [16, 4096, 4096], P('expert', 'tensor')
The draws below stay inside these ranges and needn't reach their ends.
Inputs may be any that keep to these rules, and one draw needn't show every extreme that they name: `expert_ids`: each token names two different experts. Within each aligned block of 128 tokens no expert is named by more than 68 tokens, a bound that some block reaches.
All inputs are finite; a program needn't handle non-finite values.
Results may differ from the reference program's by a relative error of at most 0.019.
Values may be sent and summed in bfloat16 or wider, within the bound.
No kernel may reach another device: no remote copies, remote signals or barrier semaphores. Data moves between devices by JAX's collectives and lax.ppermute only.
A program may use at most 192 MiB of HBM per device.

```python
import math
from functools import partial
import jax
import jax.numpy as jnp
import numpy as np
from jax import lax

D = 4096
HID = 16384
TOPK = 2
SPREAD = 4
TOK_GROUP = 128
EXPERTS = 4
SLAB = 4096
CAP = 68
TOKENS = 2048
N_EXPERT = 16
N_TENSOR = 8


def level_of(rng, extent, shards, low, largest):
    level = 1.0
    for position, parts in shards:
        steps = jax.random.uniform(jax.random.fold_in(jax.random.fold_in(rng, 6), position), (parts,), jnp.float32, low / len(shards), largest / len(shards))
        level = level * jnp.repeat(jnp.exp(steps), extent[position] // parts).reshape((-1,) + (1,) * (len(extent) - 1 - position))
    return level


def routed_block(stream_key, own, number, rows, amount, top, limit, lean):
    ranking = jax.random.permutation(stream_key, amount)
    packed, usual = load_shares(amount, rows * top, limit, lean, True), load_shares(amount, rows * top, limit, lean, False)
    places = jnp.arange(amount)

    def named(tallies, offset_by):
        used = int((tallies > 0).sum())
        fixed = max(1, used // 4)
        shifted = fixed + (places - fixed + offset_by * (used - fixed)) % max(1, amount - fixed)
        return jnp.zeros((amount,), jnp.int32).at[ranking[jnp.where(places < fixed, places, shifted)]].set(jnp.asarray(tallies, jnp.int32))

    tallies = jnp.where(number % 4 == 0, named(packed, number // 4), named(usual, number - number // 4 - 1))
    mixed = jax.random.permutation(jax.random.fold_in(own, 3), amount)
    source_of, sink = mixed[0:amount // 2 * 2:2], mixed[1:amount // 2 * 2:2]
    room = jnp.minimum(tallies[source_of] - 1, limit - tallies[sink]) // 2
    room = jnp.where((source_of == ranking[0]) | (sink == ranking[0]) | (tallies[sink] == 0), 0, jnp.maximum(room, 0))
    shifted = jax.random.randint(jax.random.fold_in(own, 4), (amount // 2,), 0, 1 << 20) % (room + 1)
    tallies = tallies.at[source_of].add(-shifted).at[sink].add(shifted)
    items = jnp.searchsorted(jnp.cumsum(tallies), jnp.arange(rows * top), side="right").astype(jnp.int32)
    listing = items.reshape(top, rows).T
    listing = listing[jax.random.permutation(jax.random.fold_in(own, 1), rows)]
    offset_by = jax.random.randint(jax.random.fold_in(own, 2), (rows, 1), 0, top)
    return jnp.take_along_axis(listing, (jnp.arange(top)[None, :] + offset_by) % top, axis=1)


def load_shares(count, total, bound, skew, full):
    loads = [(1 << 20) // math.isqrt(standing ** skew) + 1 for standing in range(1, count + 1)]
    largest = bound if full else min(bound, max(-(-total // count), total * loads[0] // sum(loads)))
    least = 1 if total - largest >= count - 1 else 0
    counts, surplus = [largest] + [least] * (count - 1), total - largest - least * (count - 1)
    while surplus > 0:
        movable = [i for i in range(1, count) if counts[i] < largest] or [i for i in range(1, count) if counts[i] < bound]
        mass, budget = sum([loads[i] for i in movable]), surplus
        for i in movable:
            extra = min(bound - counts[i], max(1, budget * loads[i] // mass), surplus)
            counts[i] = counts[i] + extra
            surplus = surplus - extra
    return np.array(counts)


def bell_draw(key, extent, scale, reach, shards=(), held_as=jnp.bfloat16):
    values = scale * jax.random.normal(key, extent, jnp.float32)
    if shards:
        values = values * level_of(key, extent, shards, -0.22, 0.18)
    return jnp.clip(values, -reach, reach).astype(held_as)


def setup_inputs(seed: int = 0) -> dict:
    arg_keys = jax.random.split(jax.random.key(seed), 7)
    tokens = bell_draw(arg_keys[0], (TOKENS, D), 1.0, 6.0, ((0, 16), (1, 8)))
    gates = jnp.clip(0.1 + 0.79999997 * jax.random.uniform(arg_keys[1], (TOKENS, TOPK), jnp.float32) ** level_of(arg_keys[1], (TOKENS, TOPK), ((0, 16),), -0.2, 0.2), 0.1, 0.9)
    expert_ids_keys = jax.random.split(jax.random.fold_in(arg_keys[2], 1), TOKENS // TOK_GROUP)
    expert_ids_turns = jax.random.permutation(jax.random.fold_in(arg_keys[2], 3), TOKENS // TOK_GROUP)
    expert_ids = jax.vmap(lambda own, number: routed_block(jax.random.fold_in(arg_keys[2], 2), own, number, TOK_GROUP, EXPERTS, TOPK, CAP, 2))(expert_ids_keys, expert_ids_turns).reshape((TOKENS, TOPK))
    w_in = bell_draw(arg_keys[3], (EXPERTS * SPREAD, D, SLAB), D ** -0.5, 0.09375, ((0, 16), (2, 8)))
    w_out = bell_draw(arg_keys[4], (EXPERTS * SPREAD, SLAB, D), HID ** -0.5, 0.046875, ((0, 16), (1, 8)))
    out_grad = bell_draw(arg_keys[5], (TOKENS, D), 1.0, 6.0, ((0, 16), (1, 8)))
    return dict(tokens=tokens, gates=gates, expert_ids=expert_ids, w_in=w_in, w_out=w_out, out_grad=out_grad)


GELU_C = 0.7978845608028654
GELU_K = 0.044715


def gelu_value(pre_act):
    inner = GELU_C * (pre_act + GELU_K * pre_act * pre_act * pre_act)
    return 0.5 * pre_act * (1.0 + jnp.tanh(inner))


def gelu_slope(pre_act):
    inner = GELU_C * (pre_act + GELU_K * pre_act * pre_act * pre_act)
    tanh_val = jnp.tanh(inner)
    return 0.5 * (1.0 + tanh_val) + 0.5 * pre_act * (1.0 - tanh_val * tanh_val) * GELU_C * (1.0 + 3.0 * GELU_K * pre_act * pre_act)


def route_table(expert_ids, experts, capacity):
    routed = expert_ids.reshape(-1).astype(jnp.int32)
    one_hot = (routed[:, None] == jnp.arange(experts, dtype=jnp.int32)[None, :]).astype(jnp.int32)
    running = jnp.cumsum(one_hot, axis=0).astype(jnp.int32) * one_hot
    slot_of = (jnp.sum(running, axis=1) - 1).astype(jnp.int32)
    row_order = jnp.arange(routed.shape[0], dtype=jnp.int32)
    slot_rows = jnp.zeros((experts, capacity), jnp.int32).at[routed, slot_of].set(row_order)
    slot_used = jnp.zeros((experts, capacity), jnp.int32).at[routed, slot_of].set(1)
    return routed, slot_of, slot_rows, slot_used


def reference(tokens, gates, expert_ids, w_in, w_out, out_grad):
    groups = N_EXPERT
    blocks = SPREAD * N_TENSOR
    width = HID // blocks
    ids_grouped = expert_ids.reshape(groups, TOK_GROUP * TOPK)
    routed, slot_of, slot_rows, slot_used = jax.vmap(partial(route_table, experts=EXPERTS, capacity=CAP))(ids_grouped)
    tok_grouped = tokens.reshape(groups, TOK_GROUP, D)
    grad_grouped = out_grad.reshape(groups, TOK_GROUP, D)
    gate_grouped = gates.reshape(groups, TOK_GROUP * TOPK)
    group_index = jnp.arange(groups, dtype=jnp.int32)[:, None, None]
    token_index = slot_rows // TOPK
    used = slot_used[..., None] > 0
    x_rows = jnp.where(used, tok_grouped[group_index, token_index], jnp.zeros((), jnp.bfloat16)).astype(jnp.bfloat16)
    scale = gate_grouped[group_index, slot_rows] * slot_used.astype(jnp.float32)
    d_rows = (grad_grouped[group_index, token_index].astype(jnp.float32) * scale[..., None]).astype(jnp.bfloat16)
    x_by = jnp.transpose(x_rows, (1, 0, 2, 3)).reshape(EXPERTS, groups * CAP, D)
    d_by = jnp.transpose(d_rows, (1, 0, 2, 3)).reshape(EXPERTS, groups * CAP, D)
    w_first = jnp.transpose(w_in.reshape(EXPERTS, SPREAD, D, SLAB), (0, 2, 1, 3)).reshape(EXPERTS, D, HID)
    w_second = w_out.reshape(EXPERTS, HID, D)

    def one_expert(operands):
        x_part, d_part, first, second = operands
        pre_act = jnp.dot(x_part, first, preferred_element_type=jnp.float32)
        hidden = gelu_value(pre_act).astype(jnp.bfloat16)
        grad_hidden = jnp.dot(d_part, second.T, preferred_element_type=jnp.float32)
        grad_pre = (grad_hidden * gelu_slope(pre_act)).astype(jnp.bfloat16)
        second_grad = jnp.dot(hidden.T, d_part, preferred_element_type=jnp.float32).astype(jnp.bfloat16)
        first_grad = jnp.dot(x_part.T, grad_pre, preferred_element_type=jnp.float32).astype(jnp.bfloat16)

        def add_block(block, carry):
            out_acc, back_acc = carry
            start = (block * width).astype(jnp.int32)
            h_part = lax.dynamic_slice_in_dim(hidden, start, width, 1)
            g_part = lax.dynamic_slice_in_dim(grad_pre, start, width, 1)
            w2_part = lax.dynamic_slice_in_dim(second, start, width, 0)
            w1_part = lax.dynamic_slice_in_dim(first, start, width, 1)
            out_term = lax.optimization_barrier(jnp.dot(h_part, w2_part, preferred_element_type=jnp.float32).astype(jnp.bfloat16))
            back_term = lax.optimization_barrier(jnp.dot(g_part, w1_part.T, preferred_element_type=jnp.float32).astype(jnp.bfloat16))
            return (out_acc + out_term.astype(jnp.float32), back_acc + back_term.astype(jnp.float32))

        empty = jnp.zeros((x_part.shape[0], D), jnp.float32)
        out_acc, back_acc = lax.fori_loop(0, blocks, add_block, (empty, empty))
        return out_acc, back_acc, first_grad, second_grad

    out_all, back_all, first_grads, second_grads = lax.map(one_expert, (x_by, d_by, w_first, w_second))
    out_all = out_all.reshape(EXPERTS, groups, CAP, D)
    back_all = back_all.reshape(EXPERTS, groups, CAP, D)
    group_col = jnp.arange(groups, dtype=jnp.int32)[:, None]
    token_out = out_all[routed, group_col, slot_of].reshape(TOKENS, TOPK, D)
    token_back = back_all[routed, group_col, slot_of].reshape(TOKENS, TOPK, D)
    combined = jnp.einsum("tkf,tk->tf", token_out, gates, precision=lax.Precision.HIGHEST).astype(jnp.bfloat16)
    gate_grad = jnp.einsum("tkf,tf->tk", token_out, out_grad.astype(jnp.float32), precision=lax.Precision.HIGHEST)
    token_grad = jnp.sum(token_back, axis=1).astype(jnp.bfloat16)
    w_in_grad = jnp.transpose(first_grads.reshape(EXPERTS, D, SPREAD, SLAB), (0, 2, 1, 3)).reshape(EXPERTS * SPREAD, D, SLAB)
    w_out_grad = second_grads.reshape(EXPERTS * SPREAD, SLAB, D)
    return combined, token_grad, gate_grad, w_in_grad, w_out_grad
```

```python
import functools

import jax
import jax.numpy as jnp
from jax import lax
from jax.experimental import pallas as pl
from jax.experimental.pallas import tpu as pltpu
from jax.sharding import Mesh, PartitionSpec as P

CAP = 68
ROWS = 4 * CAP
HALF = 256
X = ("xh", "xl")

GELU_C = 0.7978845608028654
GELU_K = 0.044715
BF = jnp.bfloat16
F32 = jnp.float32
ANY = pl.BlockSpec(memory_space=pl.ANY)
SMEM = pl.BlockSpec(memory_space=pltpu.SMEM)
VMEM = pl.BlockSpec(memory_space=pltpu.VMEM)


def swap(value, axis, j):
    size = 2 if axis == "c" else 4
    return lax.ppermute(value, axis, [(i, i ^ j) for i in range(size)])


def call(kernel, name, outs, out_specs, in_specs, scratch, flops, moved, args):
    return pl.pallas_call(
        kernel,
        name=name,
        out_shape=outs,
        in_specs=in_specs,
        out_specs=out_specs,
        scratch_shapes=scratch,
        compiler_params=pltpu.CompilerParams(vmem_limit_bytes=56 * 1024 * 1024),
        cost_estimate=pl.CostEstimate(flops=flops, bytes_accessed=moved, transcendentals=0),
    )(*args)


def route_masks(meta, ids):
    y = meta[2]
    rank = lax.broadcasted_iota(jnp.int32, (8, 128), 0)
    expert = jnp.bitwise_xor(rank, y)
    first = ids[0:1, :] == expert
    second = ids[1:2, :] == expert
    member = jnp.where(first | second, 1.0, 0.0).astype(F32)
    earlier = lax.broadcasted_iota(jnp.int32, (128, 128), 0) < lax.broadcasted_iota(jnp.int32, (128, 128), 1)
    slot = jnp.dot(member.astype(BF), jnp.where(earlier, 1.0, 0.0).astype(BF), preferred_element_type=F32)
    slot = jnp.where(member > 0.0, slot, -1.0)
    row = lax.broadcasted_iota(jnp.int32, (ROWS, 128), 0)
    part = (row >= CAP).astype(jnp.int32) + (row >= 2 * CAP).astype(jnp.int32) + (row >= 3 * CAP).astype(jnp.int32)
    place = (row - CAP * part).astype(F32)

    def by_part(table):
        out = jnp.broadcast_to(table[0:1, :], (ROWS, 128))
        for j in range(1, 4):
            out = jnp.where(part == j, jnp.broadcast_to(table[j : j + 1, :], (ROWS, 128)), out)
        return out

    used = by_part(slot) == place
    return used, by_part(first.astype(F32)) > 0.0, by_part(second.astype(F32)) > 0.0


def select_kernel(meta, ids, gates, tokens, out_grad, x_out, d_out):
    used, first, second = route_masks(meta, ids)
    pick = jnp.where(used, 1.0, 0.0).astype(BF)
    weight = jnp.where(used & first, gates[0:1, :], 0.0) + jnp.where(used & second, gates[1:2, :], 0.0)
    scale = jnp.sum(weight, axis=1, keepdims=True)
    x_out[...] = jnp.dot(pick, tokens[...], preferred_element_type=F32).astype(BF)
    d_out[...] = (jnp.dot(pick, out_grad[...], preferred_element_type=F32) * scale).astype(BF)


def over_rows(mask, values):
    pick = jnp.where(mask, 1.0, 0.0).astype(BF)
    return lax.dot_general(pick, values, (((0,), (0,)), ((), ())), preferred_element_type=F32)


def combine_kernel(meta, ids, gates, out_grad, result, combined, gate_part):
    used, first, second = route_masks(meta, ids)
    values = result[...]
    grad = out_grad[...].astype(F32)
    total = jnp.zeros((128, 512), F32)
    for k, mask in enumerate((used & first, used & second)):
        rows = over_rows(mask, values)
        gate = jnp.transpose(jnp.broadcast_to(gates[k : k + 1, :], (128, 128)))[:, 0:1]
        total = total + rows * gate
        part = jnp.sum(rows * grad, axis=1, keepdims=True)
        gate_part[k : k + 1, :] = jnp.transpose(jnp.broadcast_to(part, (128, 128)))[0:1, :]
    combined[...] = total.astype(BF)


def token_grad_kernel(meta, ids, result, token_grad):
    used, _, _ = route_masks(meta, ids)
    token_grad[...] = over_rows(used, result[...]).astype(BF)


def piece_places(meta, pieces, jz):
    for jx in range(4):
        for half in range(2):
            source = pieces[jz].at[jx] if half == 0 else pieces[4 + jx].at[jz]
            column = jnp.bitwise_xor(meta[1], jx & 1) * 512 + half * HALF
            yield source, (jx >> 1) * ROWS, pl.multiple_of(column, HALF)


def fetch_pieces(meta, pieces, target, base, sems, jz):
    copies = []
    for n, (source, row, column) in enumerate(piece_places(meta, pieces, jz)):
        copies.append(
            pltpu.make_async_copy(source, target.at[jz, pl.ds(base + row, ROWS), pl.ds(column, HALF)], sems.at[jz, n])
        )
    return copies


def send_pieces(meta, pieces, source, sems, jz):
    copies = []
    for n, (target, row, column) in enumerate(piece_places(meta, pieces, jz)):
        copies.append(
            pltpu.make_async_copy(source.at[jz, pl.ds(row, ROWS), pl.ds(column, HALF)], target, sems.at[jz, n])
        )
    return copies


def z_block(meta, jz):
    return pl.ds(pl.multiple_of(jnp.bitwise_xor(meta[0], jz) * 1024, 1024), 1024)


def fetch_weight(meta, weight, target, sems, jz, by_rows):
    source = weight.at[z_block(meta, jz), :] if by_rows else weight.at[:, z_block(meta, jz)]
    return pltpu.make_async_copy(source, target.at[jz], sems.at[jz])


def gelu_parts(pre):
    square = pre * pre
    inner = GELU_C * (pre + GELU_K * square * pre)
    tanh = jnp.tanh(inner)
    value = 0.5 * pre * (1.0 + tanh)
    slope = 0.5 * (1.0 + tanh) + 0.5 * pre * (1.0 - tanh * tanh) * GELU_C * (1.0 + 3.0 * GELU_K * square)
    return value, slope


def rows_in_kernel(backward, meta, weight, *refs):
    if backward:
        slope_in, *pieces = refs[:9]
        out, rows, held, total, row_sems, weight_sems = refs[9:]
    else:
        pieces = refs[:8]
        hidden_out, slope_out, rows, held, total, row_sems, weight_sems = refs[8:]
    waits = []
    for jz in range(4):
        copies = [fetch_weight(meta, weight, held, weight_sems, jz, not backward)]
        copies += fetch_pieces(meta, pieces, rows, 0, row_sems, jz)
        for copy in copies:
            copy.start()
        waits.append(copies)
    dims = (((1,), (1,)), ((), ())) if backward else (((1,), (0,)), ((), ()))
    for jz in range(4):
        for copy in waits[jz]:
            copy.wait()
        term = lax.dot_general(rows[jz], held[jz], dims, preferred_element_type=F32)
        if jz == 0:
            total[...] = term
        else:
            total[...] += term
    if backward:
        out[...] = (total[...] * slope_in[...]).astype(BF)
    else:
        value, slope = gelu_parts(total[...])
        hidden_out[...] = value.astype(BF)
        slope_out[...] = slope


def rows_in(meta, weight, pieces, slope=None):
    backward = slope is not None
    wide = jax.ShapeDtypeStruct((2 * ROWS, 512), BF)
    chunk = (4, 512, 1024) if backward else (4, 1024, 512)
    return call(
        functools.partial(rows_in_kernel, backward),
        "grad_hidden" if backward else "hidden",
        wide if backward else (wide, jax.ShapeDtypeStruct((2 * ROWS, 512), F32)),
        VMEM if backward else (VMEM, VMEM),
        [SMEM, ANY] + ([VMEM] if backward else []) + [ANY] * 8,
        [
            pltpu.VMEM((4, 2 * ROWS, 1024), BF),
            pltpu.VMEM(chunk, BF),
            pltpu.VMEM((2 * ROWS, 512), F32),
            pltpu.SemaphoreType.DMA((4, 8)),
            pltpu.SemaphoreType.DMA((4,)),
        ],
        2 * 2 * ROWS * 4096 * 512,
        10 * 1024 * 1024,
        [meta, weight] + ([slope] if backward else []) + list(pieces),
    )


def rows_out_kernel(backward, adding, meta, weight, source, *refs):
    if adding:
        (arrived, *pieces), rest = refs[:9], refs[9:]
        held, made, other, row_sems, weight_sems, other_sems = rest
        incoming = [arrived.at[i] for i in range(8)]
    else:
        arrived, held, made, row_sems, weight_sems = refs
        pieces = [arrived.at[i] for i in range(8)]
    waits = []
    for jz in range(4):
        copies = [fetch_weight(meta, weight, held, weight_sems, jz, backward)]
        if adding:
            copies += fetch_pieces(meta, incoming, other, 0, other_sems, jz)
        for copy in copies:
            copy.start()
        waits.append(copies)
    dims = (((1,), (1,)), ((), ())) if backward else (((1,), (0,)), ((), ()))
    sent = []
    for jz in range(4):
        for copy in waits[jz]:
            copy.wait()
        term = lax.dot_general(source[...], held[jz], dims, preferred_element_type=F32)
        if adding:
            term = term + other[jz].astype(F32)
        made[jz] = term.astype(BF)
        for copy in send_pieces(meta, pieces, made, row_sems, jz):
            copy.start()
            sent.append(copy)
    for copy in sent:
        copy.wait()


def rows_out(meta, weight, source, backward, arrived=None):
    adding = arrived is not None
    piece = jax.ShapeDtypeStruct((4, ROWS, HALF), BF)
    chunk = (4, 1024, 512) if backward else (4, 512, 1024)
    block = pltpu.VMEM((4, 2 * ROWS, 1024), BF)
    return call(
        functools.partial(rows_out_kernel, backward, adding),
        ("back" if backward else "out") + ("_own" if adding else "_other"),
        (piece,) * 8 if adding else jax.ShapeDtypeStruct((8, 4, ROWS, HALF), BF),
        (ANY,) * 8 if adding else ANY,
        [SMEM, ANY, VMEM] + ([ANY] if adding else []),
        [pltpu.VMEM(chunk, BF), block]
        + ([block] if adding else [])
        + [pltpu.SemaphoreType.DMA((4, 8)), pltpu.SemaphoreType.DMA((4,))]
        + ([pltpu.SemaphoreType.DMA((4, 8))] if adding else []),
        2 * 2 * ROWS * 4096 * 512,
        (14 if adding else 10) * 1024 * 1024,
        [meta, weight, source] + ([arrived] if adding else []),
    )


def weight_grad_kernel(first, meta, own, other, *refs):
    pieces, (out, rows, made, row_sems, out_sems) = refs[:16], refs[16:]
    waits = []
    for jz in range(4):
        copies = fetch_pieces(meta, pieces[:8], rows, 0, row_sems.at[0], jz)
        copies += fetch_pieces(meta, pieces[8:], rows, 2 * ROWS, row_sems.at[1], jz)
        for copy in copies:
            copy.start()
        waits.append(copies)
    sides = jnp.concatenate([own[...], other[...]], axis=0)
    dims = (((0,), (0,)), ((), ()))
    sent = []
    for jz in range(4):
        for copy in waits[jz]:
            copy.wait()
        if first:
            term = lax.dot_general(rows[jz], sides, dims, preferred_element_type=F32)
            target = out.at[z_block(meta, jz), :]
        else:
            term = lax.dot_general(sides, rows[jz], dims, preferred_element_type=F32)
            target = out.at[:, z_block(meta, jz)]
        made[jz] = term.astype(BF)
        copy = pltpu.make_async_copy(made.at[jz], target, out_sems.at[jz])
        copy.start()
        sent.append(copy)
    for copy in sent:
        copy.wait()


def weight_grad(meta, first, own, other, pieces):
    return call(
        functools.partial(weight_grad_kernel, first),
        "w_in_grad" if first else "w_out_grad",
        jax.ShapeDtypeStruct((4096, 512) if first else (512, 4096), BF),
        ANY,
        [SMEM, VMEM, VMEM] + [ANY] * 16,
        [
            pltpu.VMEM((4, 4 * ROWS, 1024), BF),
            pltpu.VMEM((4, 1024, 512) if first else (4, 512, 1024), BF),
            pltpu.SemaphoreType.DMA((2, 4, 8)),
            pltpu.SemaphoreType.DMA((4,)),
        ],
        2 * 4 * ROWS * 4096 * 512,
        14 * 1024 * 1024,
        [meta, own, other] + list(pieces),
    )


def to_experts(rows):
    parts = [rows[CAP * j : CAP * (j + 1)] for j in range(4)]
    return jnp.concatenate([parts[0]] + [swap(parts[j], "y", j) for j in range(1, 4)], axis=0)


def gather(rows):
    stage = []
    for half, axis in ((0, X), (1, "z")):
        part = rows[:, half * HALF : (half + 1) * HALF]
        stage.append(jnp.stack([part] + [swap(part, axis, j) for j in range(1, 4)]))
    own = []
    for block, axis in zip(stage, ("z", X)):
        own += [block] + [swap(block, axis, j) for j in range(1, 4)]
    return own, [swap(piece, "c", 1) for piece in own]


def reduce_pieces(pieces):
    halves = []
    for half, axes in ((0, ("z", X)), (1, (X, "z"))):
        mine = pieces[4 * half : 4 * half + 4]
        arrived = [mine[0]] + [swap(mine[j], axes[0], j) for j in range(1, 4)]
        parts = [sum(a[i].astype(F32) for a in arrived).astype(BF) for i in range(4)]
        arrived = [parts[0]] + [swap(parts[j], axes[1], j) for j in range(1, 4)]
        halves.append(sum(a.astype(F32) for a in arrived).astype(BF))
    return jnp.concatenate(halves, axis=1)


def local(tokens, gates, expert_ids, w_in, w_out, out_grad):
    meta = jnp.stack([lax.axis_index("z"), lax.axis_index("xl"), lax.axis_index("y")]).astype(jnp.int32)
    ids = expert_ids.T
    gates_t = gates.T
    w_first, w_second = w_in[0], w_out[0]
    rows = jax.ShapeDtypeStruct((ROWS, 512), BF)
    x_rows, d_rows = call(
        select_kernel, "select", (rows, rows), (VMEM, VMEM), [SMEM] + [VMEM] * 4, [], 10**8, 10**6,
        [meta, ids, gates_t, tokens, out_grad],
    )
    x_own, x_other = gather(to_experts(x_rows))
    d_own, d_other = gather(to_experts(d_rows))

    hidden_own, slope_own = rows_in(meta, w_first, x_own)
    hidden_other, slope_other = rows_in(meta, w_first, x_other)
    out_other = swap(rows_out(meta, w_second, hidden_other, False), "c", 1)
    out_result = to_experts(reduce_pieces(rows_out(meta, w_second, hidden_own, False, out_other)))

    grad_own = rows_in(meta, w_second, d_own, slope_own)
    grad_other = rows_in(meta, w_second, d_other, slope_other)
    back_other = swap(rows_out(meta, w_first, grad_other, True), "c", 1)
    back_result = to_experts(reduce_pieces(rows_out(meta, w_first, grad_own, True, back_other)))

    w_out_grad = weight_grad(meta, False, hidden_own, hidden_other, d_own + d_other)
    w_in_grad = weight_grad(meta, True, grad_own, grad_other, x_own + x_other)

    combined, gate_part = call(
        combine_kernel, "combine",
        (jax.ShapeDtypeStruct((128, 512), BF), jax.ShapeDtypeStruct((2, 128), F32)), (VMEM, VMEM),
        [SMEM] + [VMEM] * 4, [], 10**8, 10**6, [meta, ids, gates_t, out_grad, out_result],
    )
    for axis, j in (("z", 1), ("z", 2), (X, 1)):
        gate_part = gate_part + swap(gate_part, axis, j)
    token_grad = call(
        token_grad_kernel, "token_grad", jax.ShapeDtypeStruct((128, 512), BF), VMEM,
        [SMEM] + [VMEM] * 2, [], 10**8, 10**6, [meta, ids, back_result],
    )
    return combined, token_grad, gate_part.T, w_in_grad[None], w_out_grad[None]


def solution(mesh):
    fine = Mesh(mesh.devices.reshape(4, 2, 2, 4, 2), ("y", "xh", "c", "z", "xl"))
    expert, tensor = ("y", "xh", "c"), ("z", "xl")
    return jax.shard_map(
        local,
        mesh=fine,
        in_specs=(
            P(expert, tensor),
            P(expert, None),
            P(expert, None),
            P(expert, None, tensor),
            P(expert, tensor, None),
            P(expert, tensor),
        ),
        out_specs=(
            P(expert, tensor),
            P(expert, tensor),
            P(expert, None),
            P(expert, None, tensor),
            P(expert, tensor, None),
        ),
        check_vma=False,
    )
```

```python
import functools

import jax
import jax.numpy as jnp
from jax import lax
from jax.experimental import pallas as pl
from jax.experimental.pallas import tpu as pltpu
from jax.sharding import Mesh, PartitionSpec as P

CAP = 68
ROWS = 4 * CAP
PAIR = 2 * ROWS
HALF = 256
X = ("xh", "xl")

GELU_C = 0.7978845608028654
GELU_K = 0.044715
BF = jnp.bfloat16
F32 = jnp.float32
ANY = pl.BlockSpec(memory_space=pl.ANY)
SMEM = pl.BlockSpec(memory_space=pltpu.SMEM)
VMEM = pl.BlockSpec(memory_space=pltpu.VMEM)


def swap(value, axis, j):
    size = 2 if axis == "c" else 4
    return lax.ppermute(value, axis, [(i, i ^ j) for i in range(size)])


def call(kernel, name, outs, out_specs, in_specs, scratch, flops, moved, args, limit=32):
    return pl.pallas_call(
        kernel,
        name=name,
        out_shape=outs,
        in_specs=in_specs,
        out_specs=out_specs,
        scratch_shapes=scratch,
        compiler_params=pltpu.CompilerParams(vmem_limit_bytes=limit * 1024 * 1024),
        cost_estimate=pl.CostEstimate(flops=flops // 16, bytes_accessed=moved // 16, transcendentals=0),
    )(*args)


def route_masks(meta, ids):
    y = meta[2]
    rank = lax.broadcasted_iota(jnp.int32, (8, 128), 0)
    expert = jnp.bitwise_xor(rank, y)
    first = ids[0:1, :] == expert
    second = ids[1:2, :] == expert
    member = jnp.where(first | second, 1.0, 0.0).astype(F32)
    earlier = lax.broadcasted_iota(jnp.int32, (128, 128), 0) < lax.broadcasted_iota(jnp.int32, (128, 128), 1)
    slot = jnp.dot(member.astype(BF), jnp.where(earlier, 1.0, 0.0).astype(BF), preferred_element_type=F32)
    slot = jnp.where(member > 0.0, slot, -1.0)
    row = lax.broadcasted_iota(jnp.int32, (ROWS, 128), 0)
    part = (row >= CAP).astype(jnp.int32) + (row >= 2 * CAP).astype(jnp.int32) + (row >= 3 * CAP).astype(jnp.int32)
    place = (row - CAP * part).astype(F32)

    def by_part(table):
        out = jnp.broadcast_to(table[0:1, :], (ROWS, 128))
        for j in range(1, 4):
            out = jnp.where(part == j, jnp.broadcast_to(table[j : j + 1, :], (ROWS, 128)), out)
        return out

    used = by_part(slot) == place
    return used, by_part(first.astype(F32)) > 0.0, by_part(second.astype(F32)) > 0.0


def select_kernel(meta, ids, gates, tokens, out_grad, out):
    used, first, second = route_masks(meta, ids)
    pick = jnp.where(used, 1.0, 0.0).astype(BF)
    weight = jnp.where(used & first, gates[0:1, :], 0.0) + jnp.where(used & second, gates[1:2, :], 0.0)
    scale = jnp.sum(weight, axis=1, keepdims=True)
    x_rows = jnp.dot(pick, tokens[...], preferred_element_type=F32).astype(BF)
    d_rows = (jnp.dot(pick, out_grad[...], preferred_element_type=F32) * scale).astype(BF)
    for half in range(2):
        part = slice(half * HALF, (half + 1) * HALF)
        out[:, 2 * part.start : 2 * part.start + HALF] = x_rows[:, part]
        out[:, 2 * part.start + HALF : 2 * part.start + 2 * HALF] = d_rows[:, part]


def over_rows(mask, values):
    pick = jnp.where(mask, 1.0, 0.0).astype(BF)
    return lax.dot_general(pick, values, (((0,), (0,)), ((), ())), preferred_element_type=F32)


def combine_kernel(meta, ids, gates, out_grad, result, combined, gate_part):
    used, first, second = route_masks(meta, ids)
    values = result[...]
    grad = out_grad[...].astype(F32)
    total = jnp.zeros((128, 512), F32)
    for k, mask in enumerate((used & first, used & second)):
        rows = over_rows(mask, values)
        gate = jnp.transpose(jnp.broadcast_to(gates[k : k + 1, :], (128, 128)))[:, 0:1]
        total = total + rows * gate
        part = jnp.sum(rows * grad, axis=1, keepdims=True)
        gate_part[k : k + 1, :] = jnp.transpose(jnp.broadcast_to(part, (128, 128)))[0:1, :]
    combined[...] = total.astype(BF)


def token_grad_kernel(meta, ids, result, token_grad):
    used, _, _ = route_masks(meta, ids)
    token_grad[...] = over_rows(used, result[...]).astype(BF)


def on_core(meta, c, action):
    @pl.when(meta[3] == c)
    def _():
        action()


def place(zr, xr, half):
    row, column = (xr >> 1) * PAIR, zr * 1024 + (xr & 1) * 512 + half * HALF
    return slice(row, row + PAIR), slice(column, column + HALF)


def fetch_pieces(meta, own, other, target, sems, zr, xr):
    waits = []
    for half in range(2):
        rows, columns = place(zr, xr, half)
        for c in range(2):
            arrays = own if half == c else other
            source = arrays[zr].at[xr] if half == 0 else arrays[xr].at[zr]
            copy = pltpu.make_async_copy(source, target.at[rows, columns], sems.at[zr, 2 * xr + half])
            on_core(meta, c, copy.start)
        waits.append(copy)
    return waits


def column_start(meta, zr, q):
    return jnp.bitwise_xor(meta[0], zr) * 1024 + jnp.bitwise_xor(meta[1], q) * 512


def fetch_weight(meta, weight, target, sems, kind, j, by_rows):
    copies = []
    for n in range(4 if kind else 2):
        start = column_start(meta, n, j & 1) + HALF if kind else column_start(meta, j, n)
        span = pl.ds(pl.multiple_of(start, HALF), HALF)
        part = slice(n * HALF, (n + 1) * HALF)
        source = weight.at[span, :] if by_rows else weight.at[:, span]
        copies.append(pltpu.make_async_copy(source, target.at[part, :] if by_rows else target.at[:, part], sems.at[n]))
    return copies


def times(left, right, right_by_rows):
    dims = (((1,), (0,)), ((), ())) if right_by_rows else (((1,), (1,)), ((), ()))
    return lax.dot_general(left, right, dims, preferred_element_type=F32)


def gelu_parts(pre):
    square = pre * pre
    inner = GELU_C * (pre + GELU_K * square * pre)
    tanh = jnp.tanh(inner)
    value = 0.5 * pre * (1.0 + tanh)
    slope = 0.5 * (1.0 + tanh) + 0.5 * pre * (1.0 - tanh * tanh) * GELU_C * (1.0 + 3.0 * GELU_K * square)
    return value, slope


def rows_in_kernel(js, backward, first, last, meta, weight, *refs):
    refs = list(refs)
    before = None if first else refs.pop(0)
    slope_in = refs.pop(0) if last and backward else None
    own, refs = refs[: len(js)], refs[len(js) :]
    other, refs = refs[: len(js)], refs[len(js) :]
    outs, (short, long, short_sems, long_sems) = refs[:-4], refs[-4:]
    copies = []
    for n, j in enumerate(js):
        copies += fetch_weight(meta, weight, short.at[n], short_sems.at[n], 0, j, not backward)
        copies += fetch_weight(meta, weight, long.at[n], long_sems.at[n], 1, j, not backward)
    for copy in copies:
        copy.start()
    for copy in copies:
        copy.wait()

    def add(kind0, kind1):
        for side in range(2):
            part = slice(side * PAIR, (side + 1) * PAIR)
            total = None if first else before[part, :]
            for n, j in enumerate(js):
                rows = jnp.concatenate([kind0[n][2 * side], kind0[n][2 * side + 1]], axis=1)
                term = times(rows, short[n], not backward)
                total = term if total is None else total + term
                if j >> 1 == side:
                    rows = jnp.concatenate([kind1[n][zr] for zr in range(4)], axis=1)
                    total = total + times(rows, long[n], not backward)
            if not last:
                outs[0][part, :] = total
            elif backward:
                outs[0][part, :] = (total * slope_in[part, :]).astype(BF)
            else:
                value, slope = gelu_parts(total)
                outs[0][part, :] = value.astype(BF)
                outs[1][part, :] = slope

    on_core(meta, 0, lambda: add(own, other))
    on_core(meta, 1, lambda: add(other, own))


def rows_in(js, meta, weight, own, other, before=None, slope=None, last=False, backward=False):
    first = before is None
    wide = jax.ShapeDtypeStruct((2 * PAIR, 512), F32)
    rounded = jax.ShapeDtypeStruct((2 * PAIR, 512), BF)
    outs = wide if not last else (rounded if backward else (rounded, wide))
    extra = ([] if first else [before]) + ([slope] if slope is not None else [])
    count = len(js)
    return call(
        functools.partial(rows_in_kernel, js, backward, first, last),
        ("grad_hidden" if backward else "hidden") + "".join(str(j) for j in js),
        outs,
        (VMEM, VMEM) if last and not backward else VMEM,
        [SMEM, ANY] + [VMEM] * (len(extra) + 2 * count),
        [
            pltpu.VMEM((count, 512, 512), BF),
            pltpu.VMEM((count, 512, 1024) if backward else (count, 1024, 512), BF),
            pltpu.SemaphoreType.DMA((count, 2)),
            pltpu.SemaphoreType.DMA((count, 4)),
        ],
        count * PAIR * 4096 * 512,
        count * 4 * 1024 * 1024,
        [meta, weight] + extra + [own[j] for j in js] + [other[j] for j in js],
    )


CUT = {(1, 3): 2, (0, 2): 1}


def rows_out_kernel(js, backward, adding, meta, weight, source, *refs):
    count, cut = len(js), CUT[js]
    arrived, refs = (refs[: cut * count], refs[cut * count :]) if adding else (None, refs)
    outs, (held, sems) = refs[:-2], refs[-2:]

    def make(kind):
        width = 1024 if kind else 512
        waits = []
        for n, j in enumerate(js):
            target = held.at[n, pl.ds(0, width), :] if backward else held.at[n, :, pl.ds(0, width)]
            waits.append(fetch_weight(meta, weight, target, sems.at[n], kind, j, backward))
            for copy in waits[n]:
                copy.start()
        for n, j in enumerate(js):
            for copy in waits[n]:
                copy.wait()
            right = held[n, :width, :] if backward else held[n, :, :width]
            if kind:
                part = slice((j >> 1) * PAIR, ((j >> 1) + 1) * PAIR)
                made = times(source[part, :], right, not backward)
                blocks = [made[:, zr * HALF : (zr + 1) * HALF] for zr in range(4)]
            else:
                blocks = []
                for side in range(2):
                    made = times(source[side * PAIR : (side + 1) * PAIR, :], right, not backward)
                    blocks += [made[:, :HALF], made[:, HALF:]]
            for i, block in enumerate(blocks):
                if adding:
                    outs[n][i] = (block + arrived[cut * n + i * cut // 4][i % (4 // cut)].astype(F32)).astype(BF)
                else:
                    outs[cut * n + i * cut // 4][i % (4 // cut)] = block.astype(BF)

    for c in range(2):
        on_core(meta, c, functools.partial(make, c if adding else 1 - c))


def rows_out(js, meta, weight, source, backward, arrived=None):
    adding = arrived is not None
    count, cut = len(js), CUT[js]
    made = call(
        functools.partial(rows_out_kernel, js, backward, adding),
        ("back" if backward else "out") + ("_own" if adding else "_other") + "".join(str(j) for j in js),
        (jax.ShapeDtypeStruct((4 if adding else 4 // cut, PAIR, HALF), BF),) * (count if adding else cut * count),
        (VMEM,) * (count if adding else cut * count),
        [SMEM, ANY, VMEM] + [VMEM] * (cut * count if adding else 0),
        [pltpu.VMEM((count, 1024, 512) if backward else (count, 512, 1024), BF), pltpu.SemaphoreType.DMA((count, 4))],
        count * PAIR * 1024 * 512,
        count * 3 * 1024 * 1024,
        [meta, weight, source] + ([half for j in js for half in arrived[j]] if adding else []),
    )
    return {j: made[n] if adding else made[cut * n : cut * n + cut] for n, j in enumerate(js)}


def weight_grad_kernel(first, meta, side, *refs):
    own, other, (out, rows, made, row_sems, out_sems) = refs[:4], refs[4:8], refs[8:]
    waits = []
    for zr in range(4):
        waits.append([])
        for xr in range(4):
            waits[zr] += fetch_pieces(meta, own, other, rows, row_sems, zr, xr)
    dims = (((0,), (0,)), ((), ()))
    leaving = []
    for zr in range(4):
        for copy in waits[zr]:
            copy.wait()
        block = rows[:, zr * 1024 : (zr + 1) * 1024]
        if first:
            term = lax.dot_general(block, side[...], dims, preferred_element_type=F32)
        else:
            term = lax.dot_general(side[...], block, dims, preferred_element_type=F32)
        made[zr] = term.astype(BF)
        for q in range(2):
            span = pl.ds(pl.multiple_of(column_start(meta, zr, q), 512), 512)
            part = slice(q * 512, (q + 1) * 512)
            source = made.at[zr, part, :] if first else made.at[zr, :, part]
            target = out.at[span, :] if first else out.at[:, span]
            copy = pltpu.make_async_copy(source, target, out_sems.at[zr, q])
            copy.start()
            leaving.append(copy)
    for copy in leaving:
        copy.wait()


def weight_grad(meta, first, side, own, other):
    return call(
        functools.partial(weight_grad_kernel, first),
        "w_in_grad" if first else "w_out_grad",
        jax.ShapeDtypeStruct((4096, 512) if first else (512, 4096), BF),
        ANY,
        [SMEM, VMEM] + [ANY] * 8,
        [
            pltpu.VMEM((2 * PAIR, 4096), BF),
            pltpu.VMEM((4, 1024, 512) if first else (4, 512, 1024), BF),
            pltpu.SemaphoreType.DMA((4, 8)),
            pltpu.SemaphoreType.DMA((4, 2)),
        ],
        2 * 2 * PAIR * 4096 * 512,
        14 * 1024 * 1024,
        [meta, side] + list(own) + list(other),
        limit=56,
    )


PLANE = ("xh", "c", "z", "xl")


def swap_by_core(value, stage, j):
    pairs = []
    for xh in range(2):
        for c in range(2):
            for z in range(4):
                for xl in range(2):
                    x, to_z = 2 * xh + xl, z
                    if c == stage:
                        x = x ^ j
                    else:
                        to_z = z ^ j
                    source = ((xh * 2 + c) * 4 + z) * 2 + xl
                    target = (((x >> 1) * 2 + c) * 4 + to_z) * 2 + (x & 1)
                    pairs.append((source, target))
    return lax.ppermute(value, PLANE, pairs)


def after(value, other):
    return value if other is None else lax.optimization_barrier((value, other))[0]


def to_experts(rows):
    parts = [rows[CAP * j : CAP * (j + 1)] for j in range(4)]
    return jnp.concatenate([parts[0]] + [swap(parts[j], "y", j) for j in range(1, 4)], axis=0)


def by_core(first, second, axis):
    return jnp.where(
        lax.axis_index("c") == 0,
        jnp.concatenate([first, second], axis=axis),
        jnp.concatenate([second, first], axis=axis),
    )


def first_stage(rows):
    c = lax.axis_index("c")
    mine = lax.dynamic_slice_in_dim(rows, c * 512, 512, 1)
    yours = lax.dynamic_slice_in_dim(rows, (1 - c) * 512, 512, 1)
    both = by_core(mine, swap(yours, "c", 1), 0)
    x_part, d_part = both[:, :HALF], both[:, HALF:]
    x_block = jnp.stack([x_part] + [swap_by_core(x_part, 0, j) for j in range(1, 4)])
    d_part = after(d_part, x_block)
    return x_block, jnp.stack([d_part] + [swap_by_core(d_part, 0, j) for j in range(1, 4)])


def near(block, stage):
    return {j: swap_by_core(block, stage, j) for j in (1, 3)}


def sum_first(pieces, arrived):
    arrived = [pieces[0]] + [arrived[j] for j in range(1, 4)]
    return [sum(a[i].astype(F32) for a in arrived).astype(BF) for i in range(4)]


def sum_second(parts, hold=None):
    arrived = [parts[0]] + [after(swap_by_core(parts[j], 0, j), hold) for j in range(1, 4)]
    return sum(a.astype(F32) for a in arrived).astype(BF)


def to_tokens(both):
    c = lax.axis_index("c")
    mine = lax.dynamic_slice_in_dim(both, c * ROWS, ROWS, 0)
    yours = lax.dynamic_slice_in_dim(both, (1 - c) * ROWS, ROWS, 0)
    return to_experts(by_core(mine, swap(yours, "c", 1), 1))


def across(pieces):
    return {j: jax.tree.map(lambda v: swap(v, "c", 1), value) for j, value in pieces.items()}


def ordered(pieces, other):
    return {j: after(v, other) for j, v in pieces.items()}


def local(tokens, gates, expert_ids, w_in, w_out, out_grad):
    meta = jnp.stack([lax.axis_index(name) for name in ("z", "xl", "y", "c")]).astype(jnp.int32)
    ids = expert_ids.T
    gates_t = gates.T
    w_first, w_second = w_in[0], w_out[0]
    rows = call(
        select_kernel, "select", jax.ShapeDtypeStruct((ROWS, 1024), BF), VMEM, [SMEM] + [VMEM] * 4, [], 10**8, 10**6,
        [meta, ids, gates_t, tokens, out_grad],
    )
    x_block, d_block = first_stage(to_experts(rows))

    x = {0: x_block, **near(x_block, 1)}
    x_other = across(x)
    pre = rows_in((0,), meta, w_first, x, x_other)
    pre = rows_in((1, 3), meta, w_first, x, x_other, pre)
    start = after(d_block, (x[1], x[3]))
    d = {0: d_block, **ordered(near(start, 1), pre)}
    x[2] = after(swap_by_core(after(x_block, start), 1, 2), (pre, d[1], d[3]))
    x_other[2] = swap(x[2], "c", 1)
    hidden, slope = rows_in((2,), meta, w_first, x, x_other, pre, last=True)

    d_other = across(d)
    out_far = rows_out((1, 3), meta, w_second, hidden, False)
    grad = rows_in((0,), meta, w_second, d, d_other, backward=True)
    grad = rows_in((1, 3), meta, w_second, d, d_other, after(grad, out_far), backward=True)
    out = rows_out((1, 3), meta, w_second, hidden, False, ordered(across(out_far), grad))
    out_arrived = {j: swap_by_core(out[j], 1, j) for j in (1, 3)}
    d[2] = after(swap_by_core(after(d_block, (d[1], d[3])), 1, 2), out)
    d_other[2] = swap(d[2], "c", 1)
    out_near = across(rows_out((0, 2), meta, w_second, after(hidden, d[2]), False))
    grad_pre = rows_in((2,), meta, w_second, d, d_other, grad, slope, last=True, backward=True)
    back_far = rows_out((1, 3), meta, w_first, grad_pre, True)
    out.update(rows_out((0, 2), meta, w_second, hidden, False, ordered(out_near, back_far)))
    out_arrived[2] = swap_by_core(out[2], 1, 2)

    back_near = across(rows_out((0, 2), meta, w_first, after(grad_pre, back_far), True))
    back = rows_out(
        (1, 3), meta, w_first, grad_pre, True, ordered(across(back_far), (out, out_arrived[1], out_arrived[3]))
    )
    back_arrived = {j: swap_by_core(back[j], 1, j) for j in (1, 3)}
    back.update(rows_out((0, 2), meta, w_first, grad_pre, True, ordered(back_near, back)))
    back_arrived[2] = swap_by_core(back[2], 1, 2)

    w_in_grad = weight_grad(meta, True, after(grad_pre, back), [x[j] for j in range(4)], [x_other[j] for j in range(4)])
    out_parts = sum_first(out, ordered(out_arrived, w_in_grad))
    w_out_grad = weight_grad(
        meta, False, after(hidden, (w_in_grad, out_parts, back_arrived[1], back_arrived[3])), [d[j] for j in range(4)], [d_other[j] for j in range(4)]
    )
    out_sum = sum_second(out_parts, w_out_grad)
    back_parts = sum_first(back, ordered(back_arrived, (w_out_grad, out_sum)))
    out_result = to_tokens(out_sum)
    combined, gate_part = call(
        combine_kernel, "combine",
        (jax.ShapeDtypeStruct((128, 512), BF), jax.ShapeDtypeStruct((2, 128), F32)), (VMEM, VMEM),
        [SMEM] + [VMEM] * 4, [], 10**8, 10**6, [meta, ids, gates_t, out_grad, out_result],
    )
    back_result = to_tokens(sum_second(back_parts, combined))

    gate_part = sum([swap(gate_part, "z", j) for j in range(1, 4)], gate_part)
    gate_part = gate_part + swap(gate_part, X, 1)
    token_grad = call(
        token_grad_kernel, "token_grad", jax.ShapeDtypeStruct((128, 512), BF), VMEM,
        [SMEM] + [VMEM] * 2, [], 10**8, 10**6, [meta, ids, back_result],
    )
    return combined, token_grad, gate_part.T, w_in_grad[None], w_out_grad[None]


def solution(mesh):
    fine = Mesh(mesh.devices.reshape(4, 2, 2, 4, 2), ("y", "xh", "c", "z", "xl"))
    expert, tensor = ("y", "xh", "c"), ("z", "xl")
    return jax.shard_map(
        local,
        mesh=fine,
        in_specs=(
            P(expert, tensor),
            P(expert, None),
            P(expert, None),
            P(expert, None, tensor),
            P(expert, tensor, None),
            P(expert, tensor),
        ),
        out_specs=(
            P(expert, tensor),
            P(expert, tensor),
            P(expert, None),
            P(expert, None, tensor),
            P(expert, tensor, None),
        ),
        check_vma=False,
    )
```

```python
import functools

import jax
import jax.numpy as jnp
from jax import lax
from jax.experimental import pallas as pl
from jax.experimental.pallas import tpu as pltpu
from jax.sharding import Mesh, PartitionSpec as P

CAP = 68
ROWS = 4 * CAP
PAIR = 2 * ROWS
HALF = 256
X = ("xh", "xl")

GELU_C = 0.7978845608028654
GELU_K = 0.044715
BF = jnp.bfloat16
F32 = jnp.float32
ANY = pl.BlockSpec(memory_space=pl.ANY)
SMEM = pl.BlockSpec(memory_space=pltpu.SMEM)
VMEM = pl.BlockSpec(memory_space=pltpu.VMEM)


def swap(value, axis, j):
    size = 2 if axis == "c" else 4
    return lax.ppermute(value, axis, [(i, i ^ j) for i in range(size)])


def call(kernel, name, outs, out_specs, in_specs, scratch, flops, moved, args, limit=32):
    return pl.pallas_call(
        kernel,
        name=name,
        out_shape=outs,
        in_specs=in_specs,
        out_specs=out_specs,
        scratch_shapes=scratch,
        compiler_params=pltpu.CompilerParams(vmem_limit_bytes=limit * 1024 * 1024),
        cost_estimate=pl.CostEstimate(flops=flops // 16, bytes_accessed=moved // 16, transcendentals=0),
    )(*args)


def route_masks(meta, ids):
    y = meta[2]
    rank = lax.broadcasted_iota(jnp.int32, (8, 128), 0)
    expert = jnp.bitwise_xor(rank, y)
    first = ids[0:1, :] == expert
    second = ids[1:2, :] == expert
    member = jnp.where(first | second, 1.0, 0.0).astype(F32)
    earlier = lax.broadcasted_iota(jnp.int32, (128, 128), 0) < lax.broadcasted_iota(jnp.int32, (128, 128), 1)
    slot = jnp.dot(member.astype(BF), jnp.where(earlier, 1.0, 0.0).astype(BF), preferred_element_type=F32)
    slot = jnp.where(member > 0.0, slot, -1.0)
    row = lax.broadcasted_iota(jnp.int32, (ROWS, 128), 0)
    part = (row >= CAP).astype(jnp.int32) + (row >= 2 * CAP).astype(jnp.int32) + (row >= 3 * CAP).astype(jnp.int32)
    place = (row - CAP * part).astype(F32)

    def by_part(table):
        out = jnp.broadcast_to(table[0:1, :], (ROWS, 128))
        for j in range(1, 4):
            out = jnp.where(part == j, jnp.broadcast_to(table[j : j + 1, :], (ROWS, 128)), out)
        return out

    used = by_part(slot) == place
    return used, by_part(first.astype(F32)) > 0.0, by_part(second.astype(F32)) > 0.0


def select_kernel(meta, ids, gates, tokens, out_grad, out):
    used, first, second = route_masks(meta, ids)
    pick = jnp.where(used, 1.0, 0.0).astype(BF)
    weight = jnp.where(used & first, gates[0:1, :], 0.0) + jnp.where(used & second, gates[1:2, :], 0.0)
    scale = jnp.sum(weight, axis=1, keepdims=True)
    x_rows = jnp.dot(pick, tokens[...], preferred_element_type=F32).astype(BF)
    d_rows = (jnp.dot(pick, out_grad[...], preferred_element_type=F32) * scale).astype(BF)
    for half in range(2):
        part = slice(half * HALF, (half + 1) * HALF)
        out[:, 2 * part.start : 2 * part.start + HALF] = x_rows[:, part]
        out[:, 2 * part.start + HALF : 2 * part.start + 2 * HALF] = d_rows[:, part]


def over_rows(mask, values):
    pick = jnp.where(mask, 1.0, 0.0).astype(BF)
    return lax.dot_general(pick, values, (((0,), (0,)), ((), ())), preferred_element_type=F32)


def combine_kernel(meta, ids, gates, out_grad, result, combined, gate_part):
    used, first, second = route_masks(meta, ids)
    values = result[...]
    grad = out_grad[...].astype(F32)
    total = jnp.zeros((128, 512), F32)
    for k, mask in enumerate((used & first, used & second)):
        rows = over_rows(mask, values)
        gate = jnp.transpose(jnp.broadcast_to(gates[k : k + 1, :], (128, 128)))[:, 0:1]
        total = total + rows * gate
        part = jnp.sum(rows * grad, axis=1, keepdims=True)
        gate_part[k : k + 1, :] = jnp.transpose(jnp.broadcast_to(part, (128, 128)))[0:1, :]
    combined[...] = total.astype(BF)


def token_grad_kernel(meta, ids, result, token_grad):
    used, _, _ = route_masks(meta, ids)
    token_grad[...] = over_rows(used, result[...]).astype(BF)


def on_core(meta, c, action):
    @pl.when(meta[3] == c)
    def _():
        action()


def place(zr, xr, half):
    row, column = (xr >> 1) * PAIR, zr * 1024 + (xr & 1) * 512 + half * HALF
    return slice(row, row + PAIR), slice(column, column + HALF)


def take(refs, js):
    return {j: tuple(refs.pop(0) for _ in range(2 if j == 2 else 1)) for j in js}


def block_of(piece, i):
    each = 4 // len(piece)
    return piece[i // each].at[i % each]


def fetch_pieces(meta, own, other, target, sems, zr, xr):
    waits = []
    for half in range(2):
        rows, columns = place(zr, xr, half)
        for c in range(2):
            arrays = own if half == c else other
            source = block_of(arrays[zr], xr) if half == 0 else block_of(arrays[xr], zr)
            copy = pltpu.make_async_copy(source, target.at[rows, columns], sems.at[zr, 2 * xr + half])
            on_core(meta, c, copy.start)
        waits.append(copy)
    return waits


def column_start(meta, zr, q):
    return jnp.bitwise_xor(meta[0], zr) * 1024 + jnp.bitwise_xor(meta[1], q) * 512


def fetch_weight(meta, weight, target, sems, kind, j, by_rows):
    copies = []
    for n in range(4 if kind else 2):
        start = column_start(meta, n, j & 1) + HALF if kind else column_start(meta, j, n)
        span = pl.ds(pl.multiple_of(start, HALF), HALF)
        part = slice(n * HALF, (n + 1) * HALF)
        source = weight.at[span, :] if by_rows else weight.at[:, span]
        copies.append(pltpu.make_async_copy(source, target.at[part, :] if by_rows else target.at[:, part], sems.at[n]))
    return copies


def times(left, right, right_by_rows):
    dims = (((1,), (0,)), ((), ())) if right_by_rows else (((1,), (1,)), ((), ()))
    return lax.dot_general(left, right, dims, preferred_element_type=F32)


def gelu_parts(pre):
    square = pre * pre
    inner = GELU_C * (pre + GELU_K * square * pre)
    tanh = jnp.tanh(inner)
    value = 0.5 * pre * (1.0 + tanh)
    slope = 0.5 * (1.0 + tanh) + 0.5 * pre * (1.0 - tanh * tanh) * GELU_C * (1.0 + 3.0 * GELU_K * square)
    return value, slope


def rows_in_kernel(js, backward, first, last, meta, weight, *refs):
    refs = list(refs)
    before = None if first else refs.pop(0)
    slope_in = refs.pop(0) if last and backward else None
    own, other = take(refs, js), take(refs, js)
    outs, (short, long, short_sems, long_sems) = refs[:-4], refs[-4:]
    copies = []
    for n, j in enumerate(js):
        copies += fetch_weight(meta, weight, short.at[n], short_sems.at[n], 0, j, not backward)
        copies += fetch_weight(meta, weight, long.at[n], long_sems.at[n], 1, j, not backward)
    for copy in copies:
        copy.start()
    for copy in copies:
        copy.wait()

    def add(kind0, kind1):
        for side in range(2):
            part = slice(side * PAIR, (side + 1) * PAIR)
            total = None if first else before[part, :]
            for n, j in enumerate(js):
                rows = jnp.concatenate([block_of(kind0[j], 2 * side + q)[...] for q in range(2)], axis=1)
                term = times(rows, short[n], not backward)
                total = term if total is None else total + term
                if j >> 1 == side:
                    rows = jnp.concatenate([block_of(kind1[j], zr)[...] for zr in range(4)], axis=1)
                    total = total + times(rows, long[n], not backward)
            if not last:
                outs[0][part, :] = total
            elif backward:
                outs[0][part, :] = (total * slope_in[part, :]).astype(BF)
            else:
                value, slope = gelu_parts(total)
                outs[0][part, :] = value.astype(BF)
                outs[1][part, :] = slope

    on_core(meta, 0, lambda: add(own, other))
    on_core(meta, 1, lambda: add(other, own))


def rows_in(js, meta, weight, own, other, before=None, slope=None, last=False, backward=False):
    first = before is None
    wide = jax.ShapeDtypeStruct((2 * PAIR, 512), F32)
    rounded = jax.ShapeDtypeStruct((2 * PAIR, 512), BF)
    outs = wide if not last else (rounded if backward else (rounded, wide))
    extra = ([] if first else [before]) + ([slope] if slope is not None else [])
    count = len(js)
    pieces = jax.tree.leaves([[v[j] for j in js] for v in (own, other)])
    return call(
        functools.partial(rows_in_kernel, js, backward, first, last),
        ("grad_hidden" if backward else "hidden") + "".join(str(j) for j in js),
        outs,
        (VMEM, VMEM) if last and not backward else VMEM,
        [SMEM, ANY] + [VMEM] * (len(extra) + len(pieces)),
        [
            pltpu.VMEM((count, 512, 512), BF),
            pltpu.VMEM((count, 512, 1024) if backward else (count, 1024, 512), BF),
            pltpu.SemaphoreType.DMA((count, 2)),
            pltpu.SemaphoreType.DMA((count, 4)),
        ],
        count * PAIR * 4096 * 512,
        count * 4 * 1024 * 1024,
        [meta, weight] + extra + pieces,
    )


def rows_out_kernel(js, backward, adding, passing, meta, weight, source, *refs):
    refs = list(refs)
    arrived = take(refs, js) if adding else None
    passed = (refs.pop(0), refs.pop(0)) if passing else None
    outs, (held, sems) = take(refs[:-2], js), refs[-2:]

    def make(kind):
        width = 1024 if kind else 512
        waits = []
        for n, j in enumerate(js):
            target = held.at[n, pl.ds(0, width), :] if backward else held.at[n, :, pl.ds(0, width)]
            waits.append(fetch_weight(meta, weight, target, sems.at[n], kind, j, backward))
            for copy in waits[n]:
                copy.start()
        for n, j in enumerate(js):
            for copy in waits[n]:
                copy.wait()
            right = held[n, :width, :] if backward else held[n, :, :width]
            if kind:
                part = slice((j >> 1) * PAIR, ((j >> 1) + 1) * PAIR)
                made = times(source[part, :], right, not backward)
                blocks = [made[:, zr * HALF : (zr + 1) * HALF] for zr in range(4)]
            else:
                blocks = []
                for side in range(2):
                    made = times(source[side * PAIR : (side + 1) * PAIR, :], right, not backward)
                    blocks += [made[:, :HALF], made[:, HALF:]]
            for i, block in enumerate(blocks):
                if adding:
                    block = block + block_of(arrived[j], i)[...].astype(F32)
                if passing and j == (3 if i < 2 else 1):
                    block = block + passed[i // 2][i % 2].astype(F32)
                block_of(outs[j], i)[...] = block.astype(BF)

    for c in range(2):
        on_core(meta, c, functools.partial(make, c if adding else 1 - c))


def rows_out(js, meta, weight, source, backward, arrived=None, passed=None):
    adding, passing = arrived is not None, passed is not None
    count = len(js)
    extra = (jax.tree.leaves([arrived[j] for j in js]) if adding else []) + (list(passed) if passing else [])
    shapes = [jax.ShapeDtypeStruct((2 if j == 2 else 4, PAIR, HALF), BF) for j in js for _ in range(2 if j == 2 else 1)]
    made = call(
        functools.partial(rows_out_kernel, js, backward, adding, passing),
        ("back" if backward else "out") + ("_own" if adding else "_other") + "".join(str(j) for j in js),
        tuple(shapes),
        (VMEM,) * len(shapes),
        [SMEM, ANY, VMEM] + [VMEM] * len(extra),
        [pltpu.VMEM((count, 1024, 512) if backward else (count, 512, 1024), BF), pltpu.SemaphoreType.DMA((count, 4))],
        count * PAIR * 1024 * 512,
        count * 3 * 1024 * 1024,
        [meta, weight, source] + extra,
    )
    return take(list(made), js)


def weight_grad_kernel(first, meta, side, *refs):
    refs = list(refs)
    own, other = take(refs, range(4)), take(refs, range(4))
    out, rows, made, row_sems, out_sems = refs
    waits = []
    for zr in range(4):
        waits.append([])
        for xr in range(4):
            waits[zr] += fetch_pieces(meta, own, other, rows, row_sems, zr, xr)
    dims = (((0,), (0,)), ((), ()))
    leaving = []
    for zr in range(4):
        for copy in waits[zr]:
            copy.wait()
        block = rows[:, zr * 1024 : (zr + 1) * 1024]
        if first:
            term = lax.dot_general(block, side[...], dims, preferred_element_type=F32)
        else:
            term = lax.dot_general(side[...], block, dims, preferred_element_type=F32)
        made[zr] = term.astype(BF)
        for q in range(2):
            span = pl.ds(pl.multiple_of(column_start(meta, zr, q), 512), 512)
            part = slice(q * 512, (q + 1) * 512)
            source = made.at[zr, part, :] if first else made.at[zr, :, part]
            target = out.at[span, :] if first else out.at[:, span]
            copy = pltpu.make_async_copy(source, target, out_sems.at[zr, q])
            copy.start()
            leaving.append(copy)
    for copy in leaving:
        copy.wait()


def weight_grad(meta, first, side, own, other):
    return call(
        functools.partial(weight_grad_kernel, first),
        "w_in_grad" if first else "w_out_grad",
        jax.ShapeDtypeStruct((4096, 512) if first else (512, 4096), BF),
        ANY,
        [SMEM, VMEM] + [ANY] * 10,
        [
            pltpu.VMEM((2 * PAIR, 4096), BF),
            pltpu.VMEM((4, 1024, 512) if first else (4, 512, 1024), BF),
            pltpu.SemaphoreType.DMA((4, 8)),
            pltpu.SemaphoreType.DMA((4, 2)),
        ],
        2 * 2 * PAIR * 4096 * 512,
        14 * 1024 * 1024,
        [meta, side] + jax.tree.leaves([[v[j] for j in range(4)] for v in (own, other)]),
        limit=56,
    )


PLANE = ("xh", "c", "z", "xl")


def swap_by_core(value, stage, j):
    pairs = []
    for xh in range(2):
        for c in range(2):
            for z in range(4):
                for xl in range(2):
                    x, to_z = 2 * xh + xl, z
                    if c == stage:
                        x = x ^ j
                    else:
                        to_z = z ^ j
                    source = ((xh * 2 + c) * 4 + z) * 2 + xl
                    target = (((x >> 1) * 2 + c) * 4 + to_z) * 2 + (x & 1)
                    pairs.append((source, target))
    return lax.ppermute(value, PLANE, pairs)


def after(value, other):
    return value if other is None else lax.optimization_barrier((value, other))[0]


def to_experts(rows):
    parts = [rows[CAP * j : CAP * (j + 1)] for j in range(4)]
    return jnp.concatenate([parts[0]] + [swap(parts[j], "y", j) for j in range(1, 4)], axis=0)


def by_core(first, second, axis):
    return jnp.where(
        lax.axis_index("c") == 0,
        jnp.concatenate([first, second], axis=axis),
        jnp.concatenate([second, first], axis=axis),
    )


def first_stage(rows):
    c = lax.axis_index("c")
    mine = lax.dynamic_slice_in_dim(rows, c * 512, 512, 1)
    yours = lax.dynamic_slice_in_dim(rows, (1 - c) * 512, 512, 1)
    both = by_core(mine, swap(yours, "c", 1), 0)
    x_part, d_part = both[:, :HALF], both[:, HALF:]
    x_block = jnp.stack([x_part] + [swap_by_core(x_part, 0, j) for j in range(1, 4)])
    d_part = after(d_part, x_block)
    return x_block, jnp.stack([d_part] + [swap_by_core(d_part, 0, j) for j in range(1, 4)])


def near(block, stage):
    return {j: (swap_by_core(block, stage, j),) for j in (1, 3)}


def beyond(pieces, stage):
    return (swap_by_core(pieces[3][0][:2], stage, 1), swap_by_core(pieces[1][0][2:], stage, 3))


def through(pieces, stage):
    return (swap_by_core(pieces[2][0], stage, 1), swap_by_core(pieces[2][1], stage, 3))


def sum_first(pieces, arrived):
    arrived = [pieces[0][0], arrived[1][0], arrived[3][0]]
    return [sum(a[i].astype(F32) for a in arrived).astype(BF) for i in range(4)]


def sum_second(parts, hold=None):
    arrived = [parts[0]] + [after(swap_by_core(parts[j], 0, j), hold) for j in range(1, 4)]
    return sum(a.astype(F32) for a in arrived).astype(BF)


def to_home(both):
    c = lax.axis_index("c")
    mine = lax.dynamic_slice_in_dim(both, c * ROWS, ROWS, 0)
    yours = lax.dynamic_slice_in_dim(both, (1 - c) * ROWS, ROWS, 0)
    return by_core(mine, swap(yours, "c", 1), 1)


def across(pieces):
    return jax.tree.map(lambda v: swap(v, "c", 1), pieces)


def ordered(pieces, other):
    return {j: after(v, other) for j, v in pieces.items()}


def local(tokens, gates, expert_ids, w_in, w_out, out_grad):
    meta = jnp.stack([lax.axis_index(name) for name in ("z", "xl", "y", "c")]).astype(jnp.int32)
    ids = expert_ids.T
    gates_t = gates.T
    w_first, w_second = w_in[0], w_out[0]
    rows = call(
        select_kernel, "select", jax.ShapeDtypeStruct((ROWS, 1024), BF), VMEM, [SMEM] + [VMEM] * 4, [], 10**8, 10**6,
        [meta, ids, gates_t, tokens, out_grad], limit=60,
    )
    x_block, d_block = first_stage(to_experts(rows))

    x = {0: (x_block,), **ordered(near(x_block, 1), d_block)}
    x_other = across(x)
    pre = rows_in((0,), meta, w_first, x, x_other)
    pre = rows_in((1, 3), meta, w_first, x, x_other, pre)
    d_near = near(after(d_block, (x[1], x[3])), 1)
    x[2] = after(beyond(x, 1), pre)
    x_other[2] = across(x[2])
    hidden, slope = rows_in((2,), meta, w_first, x, x_other, pre, last=True)

    out_near = rows_out((0, 2), meta, w_second, hidden, False)
    d = {0: (d_block,), **ordered(d_near, out_near)}
    d_other = across(d)
    out_far = across(rows_out((1, 3), meta, w_second, after(hidden, out_near), False))
    grad = rows_in((0,), meta, w_second, d, d_other, backward=True)
    out = rows_out((0, 2), meta, w_second, hidden, False, ordered(across(out_near), grad))
    passed = through(out, 1)
    grad = rows_in((1, 3), meta, w_second, d, d_other, after(grad, out), backward=True)
    d[2] = after(beyond(d, 1), (out, grad))
    d_other[2] = across(d[2])
    grad_pre = rows_in((2,), meta, w_second, d, d_other, grad, slope, last=True, backward=True)
    back_near = rows_out((0, 2), meta, w_first, grad_pre, True)
    out.update(rows_out((1, 3), meta, w_second, after(hidden, back_near), False, out_far, passed))
    out_arrived = {j: (swap_by_core(out[j][0], 1, j),) for j in (1, 3)}
    back_far = across(rows_out((1, 3), meta, w_first, after(grad_pre, back_near), True))
    back = rows_out((0, 2), meta, w_first, grad_pre, True, ordered(across(back_near), out))
    passed = through(ordered(back, back_far), 1)

    w_in_grad = weight_grad(meta, True, after(grad_pre, back), x, x_other)
    back.update(rows_out((1, 3), meta, w_first, grad_pre, True, back_far, after(passed, w_in_grad)))
    back_arrived = {j: (swap_by_core(back[j][0], 1, j),) for j in (1, 3)}
    out_parts = sum_first(out, ordered(out_arrived, back))
    w_out_grad = weight_grad(meta, False, after(hidden, (w_in_grad, back, out_parts)), d, d_other)
    out_sum = sum_second(out_parts, w_out_grad)
    back_parts = sum_first(back, ordered(back_arrived, w_out_grad))
    back_home = to_home(sum_second(back_parts))
    out_result = to_experts(to_home(out_sum))
    combined, gate_part = call(
        combine_kernel, "combine",
        (jax.ShapeDtypeStruct((128, 512), BF), jax.ShapeDtypeStruct((2, 128), F32)), (VMEM, VMEM),
        [SMEM] + [VMEM] * 4, [], 10**8, 10**6, [meta, ids, gates_t, out_grad, after(out_result, back_home)],
    )
    back_result = to_experts(back_home)

    gate_part = sum([swap(gate_part, "z", j) for j in range(1, 4)], gate_part)
    gate_part = gate_part + swap(gate_part, X, 1)
    token_grad = call(
        token_grad_kernel, "token_grad", jax.ShapeDtypeStruct((128, 512), BF), VMEM,
        [SMEM] + [VMEM] * 2, [], 10**8, 10**6, [meta, ids, back_result],
    )
    return combined, token_grad, gate_part.T, w_in_grad[None], w_out_grad[None]


def solution(mesh):
    fine = Mesh(mesh.devices.reshape(4, 2, 2, 4, 2), ("y", "xh", "c", "z", "xl"))
    expert, tensor = ("y", "xh", "c"), ("z", "xl")
    return jax.shard_map(
        local,
        mesh=fine,
        in_specs=(
            P(expert, tensor),
            P(expert, None),
            P(expert, None),
            P(expert, None, tensor),
            P(expert, tensor, None),
            P(expert, tensor),
        ),
        out_specs=(
            P(expert, tensor),
            P(expert, tensor),
            P(expert, None),
            P(expert, None, tensor),
            P(expert, tensor, None),
        ),
        check_vma=False,
    )
```

```python
import functools

import jax
import jax.numpy as jnp
from jax import lax
from jax.experimental import pallas as pl
from jax.experimental.pallas import tpu as pltpu
from jax.sharding import Mesh, PartitionSpec as P

CAP = 68
ROWS = 4 * CAP
PAIR = 2 * ROWS
HALF = 256
X = ("xh", "xl")

GELU_C = 0.7978845608028654
GELU_K = 0.044715
BF = jnp.bfloat16
F32 = jnp.float32
ANY = pl.BlockSpec(memory_space=pl.ANY)
SMEM = pl.BlockSpec(memory_space=pltpu.SMEM)
VMEM = pl.BlockSpec(memory_space=pltpu.VMEM)


def swap(value, axis, j):
    size = 2 if axis == "c" else 4
    return lax.ppermute(value, axis, [(i, i ^ j) for i in range(size)])


def call(kernel, name, outs, out_specs, in_specs, scratch, flops, moved, args, limit=24):
    return pl.pallas_call(
        kernel,
        name=name,
        out_shape=outs,
        in_specs=in_specs,
        out_specs=out_specs,
        scratch_shapes=scratch,
        compiler_params=pltpu.CompilerParams(vmem_limit_bytes=limit * 1024 * 1024),
        cost_estimate=pl.CostEstimate(flops=flops // 16, bytes_accessed=moved // 16, transcendentals=0),
    )(*args)


def route_masks(meta, ids):
    y = meta[2]
    rank = lax.broadcasted_iota(jnp.int32, (8, 128), 0)
    expert = jnp.bitwise_xor(rank, y)
    first = ids[0:1, :] == expert
    second = ids[1:2, :] == expert
    member = jnp.where(first | second, 1.0, 0.0).astype(F32)
    earlier = lax.broadcasted_iota(jnp.int32, (128, 128), 0) < lax.broadcasted_iota(jnp.int32, (128, 128), 1)
    slot = jnp.dot(member.astype(BF), jnp.where(earlier, 1.0, 0.0).astype(BF), preferred_element_type=F32)
    slot = jnp.where(member > 0.0, slot, -1.0)
    row = lax.broadcasted_iota(jnp.int32, (ROWS, 128), 0)
    part = (row >= CAP).astype(jnp.int32) + (row >= 2 * CAP).astype(jnp.int32) + (row >= 3 * CAP).astype(jnp.int32)
    place = (row - CAP * part).astype(F32)

    def by_part(table):
        out = jnp.broadcast_to(table[0:1, :], (ROWS, 128))
        for j in range(1, 4):
            out = jnp.where(part == j, jnp.broadcast_to(table[j : j + 1, :], (ROWS, 128)), out)
        return out

    used = by_part(slot) == place
    return used, by_part(first.astype(F32)) > 0.0, by_part(second.astype(F32)) > 0.0


def select_kernel(meta, ids, gates, tokens, out_grad, out):
    used, first, second = route_masks(meta, ids)
    pick = jnp.where(used, 1.0, 0.0).astype(BF)
    weight = jnp.where(used & first, gates[0:1, :], 0.0) + jnp.where(used & second, gates[1:2, :], 0.0)
    scale = jnp.sum(weight, axis=1, keepdims=True)
    x_rows = jnp.dot(pick, tokens[...], preferred_element_type=F32).astype(BF)
    d_rows = (jnp.dot(pick, out_grad[...], preferred_element_type=F32) * scale).astype(BF)
    for half in range(2):
        part = slice(half * HALF, (half + 1) * HALF)
        out[:, 2 * part.start : 2 * part.start + HALF] = x_rows[:, part]
        out[:, 2 * part.start + HALF : 2 * part.start + 2 * HALF] = d_rows[:, part]


def over_rows(mask, values):
    pick = jnp.where(mask, 1.0, 0.0).astype(BF)
    return lax.dot_general(pick, values, (((0,), (0,)), ((), ())), preferred_element_type=F32)


def combine_kernel(meta, ids, gates, out_grad, result, combined, gate_part):
    used, first, second = route_masks(meta, ids)
    values = result[...]
    grad = out_grad[...].astype(F32)
    total = jnp.zeros((128, 512), F32)
    for k, mask in enumerate((used & first, used & second)):
        rows = over_rows(mask, values)
        gate = jnp.transpose(jnp.broadcast_to(gates[k : k + 1, :], (128, 128)))[:, 0:1]
        total = total + rows * gate
        part = jnp.sum(rows * grad, axis=1, keepdims=True)
        gate_part[k : k + 1, :] = jnp.transpose(jnp.broadcast_to(part, (128, 128)))[0:1, :]
    combined[...] = total.astype(BF)


def token_grad_kernel(meta, ids, result, token_grad):
    used, _, _ = route_masks(meta, ids)
    token_grad[...] = over_rows(used, result[...]).astype(BF)


def on_core(meta, c, action):
    @pl.when(meta[3] == c)
    def _():
        action()


def place(zr, xr, half):
    row, column = (xr >> 1) * PAIR, zr * 1024 + (xr & 1) * 512 + half * HALF
    return slice(row, row + PAIR), slice(column, column + HALF)


def take(refs, js):
    return {j: tuple(refs.pop(0) for _ in range(2 if j == 2 else 1)) for j in js}


def block_of(piece, i):
    each = 4 // len(piece)
    return piece[i // each].at[i % each]


def fetch_pieces(meta, own, other, target, sems, zr, xr):
    waits = []
    for half in range(2):
        rows, columns = place(zr, xr, half)
        for c in range(2):
            arrays = own if half == c else other
            source = block_of(arrays[zr], xr) if half == 0 else block_of(arrays[xr], zr)
            copy = pltpu.make_async_copy(source, target.at[rows, columns], sems.at[zr, 2 * xr + half])
            on_core(meta, c, copy.start)
        waits.append(copy)
    return waits


def column_start(meta, zr, q):
    return jnp.bitwise_xor(meta[0], zr) * 1024 + jnp.bitwise_xor(meta[1], q) * 512


def weight_part(meta, weight, kind, j, by_rows):
    parts = []
    for n in range(4 if kind else 2):
        start = column_start(meta, n, j & 1) + HALF if kind else column_start(meta, j, n)
        span = pl.ds(pl.multiple_of(start, HALF), HALF)
        parts.append(weight[span, :] if by_rows else weight[:, span])
    return jnp.concatenate(parts, axis=0 if by_rows else 1)


def times(left, right, right_by_rows):
    dims = (((1,), (0,)), ((), ())) if right_by_rows else (((1,), (1,)), ((), ()))
    return lax.dot_general(left, right, dims, preferred_element_type=F32)


def gelu_parts(pre):
    square = pre * pre
    inner = GELU_C * (pre + GELU_K * square * pre)
    tanh = jnp.tanh(inner)
    value = 0.5 * pre * (1.0 + tanh)
    slope = 0.5 * (1.0 + tanh) + 0.5 * pre * (1.0 - tanh * tanh) * GELU_C * (1.0 + 3.0 * GELU_K * square)
    return value, slope


def rows_in_kernel(js, backward, first, last, meta, weight, *refs):
    refs = list(refs)
    before = None if first else refs.pop(0)
    slope_in = refs.pop(0) if last and backward else None
    own, other = take(refs, js), take(refs, js)
    outs = refs

    def add(kind0, kind1):
        for side in range(2):
            part = slice(side * PAIR, (side + 1) * PAIR)
            total = None if first else before[part, :]
            for j in js:
                rows = jnp.concatenate([block_of(kind0[j], 2 * side + q)[...] for q in range(2)], axis=1)
                term = times(rows, weight_part(meta, weight, 0, j, not backward), not backward)
                total = term if total is None else total + term
                if j >> 1 == side:
                    rows = jnp.concatenate([block_of(kind1[j], zr)[...] for zr in range(4)], axis=1)
                    total = total + times(rows, weight_part(meta, weight, 1, j, not backward), not backward)
            if not last:
                outs[0][part, :] = total
            elif backward:
                outs[0][part, :] = (total * slope_in[part, :]).astype(BF)
            else:
                value, slope = gelu_parts(total)
                outs[0][part, :] = value.astype(BF)
                outs[1][part, :] = slope

    on_core(meta, 0, lambda: add(own, other))
    on_core(meta, 1, lambda: add(other, own))


def rows_in(js, meta, weight, own, other, before=None, slope=None, last=False, backward=False):
    first = before is None
    wide = jax.ShapeDtypeStruct((2 * PAIR, 512), F32)
    rounded = jax.ShapeDtypeStruct((2 * PAIR, 512), BF)
    outs = wide if not last else (rounded if backward else (rounded, wide))
    extra = ([] if first else [before]) + ([slope] if slope is not None else [])
    count = len(js)
    pieces = jax.tree.leaves([[v[j] for j in js] for v in (own, other)])
    return call(
        functools.partial(rows_in_kernel, js, backward, first, last),
        ("grad_hidden" if backward else "hidden") + "".join(str(j) for j in js),
        outs,
        (VMEM, VMEM) if last and not backward else VMEM,
        [SMEM] + [VMEM] * (1 + len(extra) + len(pieces)),
        [],
        count * PAIR * 4096 * 512,
        count * 4 * 1024 * 1024,
        [meta, weight] + extra + pieces,
    )


def rows_out_kernel(js, backward, adding, passing, meta, weight, source, *refs):
    refs = list(refs)
    arrived = take(refs, js) if adding else None
    passed = (refs.pop(0), refs.pop(0)) if passing else None
    outs = take(refs, js)

    def make(kind):
        for j in js:
            right = weight_part(meta, weight, kind, j, backward)
            if kind:
                part = slice((j >> 1) * PAIR, ((j >> 1) + 1) * PAIR)
                made = times(source[part, :], right, not backward)
                blocks = [made[:, zr * HALF : (zr + 1) * HALF] for zr in range(4)]
            else:
                blocks = []
                for side in range(2):
                    made = times(source[side * PAIR : (side + 1) * PAIR, :], right, not backward)
                    blocks += [made[:, :HALF], made[:, HALF:]]
            for i, block in enumerate(blocks):
                if adding:
                    block = block + block_of(arrived[j], i)[...].astype(F32)
                if passing and j == (3 if i < 2 else 1):
                    block = block + passed[i // 2][i % 2].astype(F32)
                block_of(outs[j], i)[...] = block.astype(BF)

    for c in range(2):
        on_core(meta, c, functools.partial(make, c if adding else 1 - c))


def rows_out(js, meta, weight, source, backward, arrived=None, passed=None):
    adding, passing = arrived is not None, passed is not None
    count = len(js)
    extra = (jax.tree.leaves([arrived[j] for j in js]) if adding else []) + (list(passed) if passing else [])
    shapes = [jax.ShapeDtypeStruct((2 if j == 2 else 4, PAIR, HALF), BF) for j in js for _ in range(2 if j == 2 else 1)]
    made = call(
        functools.partial(rows_out_kernel, js, backward, adding, passing),
        ("back" if backward else "out") + ("_own" if adding else "_other") + "".join(str(j) for j in js),
        tuple(shapes),
        (VMEM,) * len(shapes),
        [SMEM, VMEM, VMEM] + [VMEM] * len(extra),
        [],
        count * PAIR * 1024 * 512,
        count * 3 * 1024 * 1024,
        [meta, weight, source] + extra,
    )
    return take(list(made), js)


def weight_grad_kernel(first, meta, side, *refs):
    refs = list(refs)
    own, other = take(refs, range(4)), take(refs, range(4))
    out, rows, made, row_sems, out_sems = refs
    waits = []
    for zr in range(4):
        waits.append([])
        for xr in range(4):
            waits[zr] += fetch_pieces(meta, own, other, rows, row_sems, zr, xr)
    dims = (((0,), (0,)), ((), ()))
    leaving = []
    for zr in range(4):
        for copy in waits[zr]:
            copy.wait()
        block = rows[:, zr * 1024 : (zr + 1) * 1024]
        if first:
            term = lax.dot_general(block, side[...], dims, preferred_element_type=F32)
        else:
            term = lax.dot_general(side[...], block, dims, preferred_element_type=F32)
        made[zr] = term.astype(BF)
        for q in range(2):
            span = pl.ds(pl.multiple_of(column_start(meta, zr, q), 512), 512)
            part = slice(q * 512, (q + 1) * 512)
            source = made.at[zr, part, :] if first else made.at[zr, :, part]
            target = out.at[span, :] if first else out.at[:, span]
            copy = pltpu.make_async_copy(source, target, out_sems.at[zr, q])
            copy.start()
            leaving.append(copy)
    for copy in leaving:
        copy.wait()


def weight_grad(meta, first, side, own, other):
    return call(
        functools.partial(weight_grad_kernel, first),
        "w_in_grad" if first else "w_out_grad",
        jax.ShapeDtypeStruct((4096, 512) if first else (512, 4096), BF),
        ANY,
        [SMEM, VMEM] + [ANY] * 10,
        [
            pltpu.VMEM((2 * PAIR, 4096), BF),
            pltpu.VMEM((4, 1024, 512) if first else (4, 512, 1024), BF),
            pltpu.SemaphoreType.DMA((4, 8)),
            pltpu.SemaphoreType.DMA((4, 2)),
        ],
        2 * 2 * PAIR * 4096 * 512,
        14 * 1024 * 1024,
        [meta, side] + jax.tree.leaves([[v[j] for j in range(4)] for v in (own, other)]),
        limit=56,
    )


PLANE = ("xh", "c", "z", "xl")


def swap_by_core(value, stage, j):
    pairs = []
    for xh in range(2):
        for c in range(2):
            for z in range(4):
                for xl in range(2):
                    x, to_z = 2 * xh + xl, z
                    if c == stage:
                        x = x ^ j
                    else:
                        to_z = z ^ j
                    source = ((xh * 2 + c) * 4 + z) * 2 + xl
                    target = (((x >> 1) * 2 + c) * 4 + to_z) * 2 + (x & 1)
                    pairs.append((source, target))
    return lax.ppermute(value, PLANE, pairs)


def after(value, other):
    return value if other is None else lax.optimization_barrier((value, other))[0]


def to_experts(rows):
    parts = [rows[CAP * j : CAP * (j + 1)] for j in range(4)]
    return jnp.concatenate([parts[0]] + [swap(parts[j], "y", j) for j in range(1, 4)], axis=0)


def by_core(first, second, axis):
    return jnp.where(
        lax.axis_index("c") == 0,
        jnp.concatenate([first, second], axis=axis),
        jnp.concatenate([second, first], axis=axis),
    )


def first_stage(rows):
    c = lax.axis_index("c")
    mine = lax.dynamic_slice_in_dim(rows, c * 512, 512, 1)
    yours = lax.dynamic_slice_in_dim(rows, (1 - c) * 512, 512, 1)
    both = by_core(mine, swap(yours, "c", 1), 0)
    x_part, d_part = both[:, :HALF], both[:, HALF:]
    x_block = jnp.stack([x_part] + [swap_by_core(x_part, 0, j) for j in range(1, 4)])
    d_part = after(d_part, x_block)
    return x_block, jnp.stack([d_part] + [swap_by_core(d_part, 0, j) for j in range(1, 4)])


def near(block, stage):
    return {j: (swap_by_core(block, stage, j),) for j in (1, 3)}


def beyond(pieces, stage):
    return (swap_by_core(pieces[3][0][:2], stage, 1), swap_by_core(pieces[1][0][2:], stage, 3))


def through(pieces, stage):
    return (swap_by_core(pieces[2][0], stage, 1), swap_by_core(pieces[2][1], stage, 3))


def sum_first(pieces, arrived):
    arrived = [pieces[0][0], arrived[1][0], arrived[3][0]]
    return [sum(a[i].astype(F32) for a in arrived).astype(BF) for i in range(4)]


def sum_second(parts, hold=None):
    arrived = [parts[0]] + [after(swap_by_core(parts[j], 0, j), hold) for j in range(1, 4)]
    return sum(a.astype(F32) for a in arrived).astype(BF)


def to_home(both):
    c = lax.axis_index("c")
    mine = lax.dynamic_slice_in_dim(both, c * ROWS, ROWS, 0)
    yours = lax.dynamic_slice_in_dim(both, (1 - c) * ROWS, ROWS, 0)
    return by_core(mine, swap(yours, "c", 1), 1)


def across(pieces):
    return jax.tree.map(lambda v: swap(v, "c", 1), pieces)


def ordered(pieces, other):
    return {j: after(v, other) for j, v in pieces.items()}


def local(tokens, gates, expert_ids, w_in, w_out, out_grad):
    meta = jnp.stack([lax.axis_index(name) for name in ("z", "xl", "y", "c")]).astype(jnp.int32)
    ids = expert_ids.T
    gates_t = gates.T
    w_first, w_second = w_in[0], w_out[0]
    rows = call(
        select_kernel, "select", jax.ShapeDtypeStruct((ROWS, 1024), BF), VMEM, [SMEM] + [VMEM] * 4, [], 10**8, 10**6,
        [meta, ids, gates_t, tokens, out_grad], limit=60,
    )
    x_block, d_block = first_stage(to_experts(rows))

    x = {0: (x_block,), **ordered(near(x_block, 1), d_block)}
    x_other = across(x)
    pre = rows_in((0,), meta, w_first, x, x_other)
    pre = rows_in((1, 3), meta, w_first, x, x_other, pre)
    d_near = near(after(d_block, (x[1], x[3])), 1)
    x[2] = after(beyond(x, 1), pre)
    x_other[2] = across(x[2])
    hidden, slope = rows_in((2,), meta, w_first, x, x_other, pre, last=True)

    out_near = rows_out((0, 2), meta, w_second, hidden, False)
    d = {0: (d_block,), **ordered(d_near, out_near)}
    d_other = across(d)
    out_far = across(rows_out((1, 3), meta, w_second, after(hidden, out_near), False))
    grad = rows_in((0,), meta, w_second, d, d_other, backward=True)
    out = rows_out((0, 2), meta, w_second, hidden, False, ordered(across(out_near), grad))
    passed = through(out, 1)
    grad = rows_in((1, 3), meta, w_second, d, d_other, after(grad, out), backward=True)
    d[2] = after(beyond(d, 1), (out, grad))
    d_other[2] = across(d[2])
    grad_pre = rows_in((2,), meta, w_second, d, d_other, grad, slope, last=True, backward=True)
    back_near = rows_out((0, 2), meta, w_first, grad_pre, True)
    out.update(rows_out((1, 3), meta, w_second, after(hidden, back_near), False, out_far, passed))
    out_arrived = {j: (swap_by_core(out[j][0], 1, j),) for j in (1, 3)}
    back_far = across(rows_out((1, 3), meta, w_first, after(grad_pre, back_near), True))
    back = rows_out((0, 2), meta, w_first, grad_pre, True, ordered(across(back_near), out))
    passed = through(ordered(back, back_far), 1)

    w_in_grad = weight_grad(meta, True, after(grad_pre, back), x, x_other)
    back.update(rows_out((1, 3), meta, w_first, grad_pre, True, back_far, after(passed, w_in_grad)))
    back_arrived = {j: (swap_by_core(back[j][0], 1, j),) for j in (1, 3)}
    out_parts = sum_first(out, ordered(out_arrived, back))
    w_out_grad = weight_grad(meta, False, after(hidden, (w_in_grad, back, out_parts)), d, d_other)
    out_sum = sum_second(out_parts, w_out_grad)
    back_parts = sum_first(back, ordered(back_arrived, w_out_grad))
    back_home = to_home(sum_second(back_parts))
    out_result = to_experts(to_home(out_sum))
    combined, gate_part = call(
        combine_kernel, "combine",
        (jax.ShapeDtypeStruct((128, 512), BF), jax.ShapeDtypeStruct((2, 128), F32)), (VMEM, VMEM),
        [SMEM] + [VMEM] * 4, [], 10**8, 10**6, [meta, ids, gates_t, out_grad, after(out_result, back_home)],
    )
    back_result = to_experts(back_home)

    gate_part = sum([swap(gate_part, "z", j) for j in range(1, 4)], gate_part)
    gate_part = gate_part + swap(gate_part, X, 1)
    token_grad = call(
        token_grad_kernel, "token_grad", jax.ShapeDtypeStruct((128, 512), BF), VMEM,
        [SMEM] + [VMEM] * 2, [], 10**8, 10**6, [meta, ids, back_result],
    )
    return combined, token_grad, gate_part.T, w_in_grad[None], w_out_grad[None]


def solution(mesh):
    fine = Mesh(mesh.devices.reshape(4, 2, 2, 4, 2), ("y", "xh", "c", "z", "xl"))
    expert, tensor = ("y", "xh", "c"), ("z", "xl")
    return jax.shard_map(
        local,
        mesh=fine,
        in_specs=(
            P(expert, tensor),
            P(expert, None),
            P(expert, None),
            P(expert, None, tensor),
            P(expert, tensor, None),
            P(expert, tensor),
        ),
        out_specs=(
            P(expert, tensor),
            P(expert, tensor),
            P(expert, None),
            P(expert, None, tensor),
            P(expert, tensor, None),
        ),
        check_vma=False,
    )
```

```python
import functools

import jax
import jax.numpy as jnp
from jax import lax
from jax.experimental import pallas as pl
from jax.experimental.pallas import tpu as pltpu
from jax.sharding import Mesh, PartitionSpec as P

CAP = 68
ROWS = 4 * CAP
PAIR = 2 * ROWS
HALF = 256
X = ("xh", "xl")

GELU_C = 0.7978845608028654
GELU_K = 0.044715
BF = jnp.bfloat16
F32 = jnp.float32
ANY = pl.BlockSpec(memory_space=pl.ANY)
SMEM = pl.BlockSpec(memory_space=pltpu.SMEM)
VMEM = pl.BlockSpec(memory_space=pltpu.VMEM)


def swap(value, axis, j):
    size = 2 if axis == "c" else 4
    return lax.ppermute(value, axis, [(i, i ^ j) for i in range(size)])


def call(kernel, name, outs, out_specs, in_specs, scratch, flops, moved, args, limit=24):
    return pl.pallas_call(
        kernel,
        name=name,
        out_shape=outs,
        in_specs=in_specs,
        out_specs=out_specs,
        scratch_shapes=scratch,
        compiler_params=pltpu.CompilerParams(vmem_limit_bytes=limit * 1024 * 1024),
        cost_estimate=pl.CostEstimate(flops=flops // 16, bytes_accessed=moved // 16, transcendentals=0),
    )(*args)


def route_masks(meta, ids):
    y = meta[2]
    rank = lax.broadcasted_iota(jnp.int32, (8, 128), 0)
    expert = jnp.bitwise_xor(rank, y)
    first = ids[0:1, :] == expert
    second = ids[1:2, :] == expert
    member = jnp.where(first | second, 1.0, 0.0).astype(F32)
    earlier = lax.broadcasted_iota(jnp.int32, (128, 128), 0) < lax.broadcasted_iota(jnp.int32, (128, 128), 1)
    slot = jnp.dot(member.astype(BF), jnp.where(earlier, 1.0, 0.0).astype(BF), preferred_element_type=F32)
    slot = jnp.where(member > 0.0, slot, -1.0)
    row = lax.broadcasted_iota(jnp.int32, (ROWS, 128), 0)
    part = (row >= CAP).astype(jnp.int32) + (row >= 2 * CAP).astype(jnp.int32) + (row >= 3 * CAP).astype(jnp.int32)
    place = (row - CAP * part).astype(F32)

    def by_part(table):
        out = jnp.broadcast_to(table[0:1, :], (ROWS, 128))
        for j in range(1, 4):
            out = jnp.where(part == j, jnp.broadcast_to(table[j : j + 1, :], (ROWS, 128)), out)
        return out

    used = by_part(slot) == place
    return used, by_part(first.astype(F32)) > 0.0, by_part(second.astype(F32)) > 0.0


def select_kernel(meta, ids, gates, tokens, out_grad, out):
    used, first, second = route_masks(meta, ids)
    pick = jnp.where(used, 1.0, 0.0).astype(BF)
    weight = jnp.where(used & first, gates[0:1, :], 0.0) + jnp.where(used & second, gates[1:2, :], 0.0)
    scale = jnp.sum(weight, axis=1, keepdims=True)
    x_rows = jnp.dot(pick, tokens[...], preferred_element_type=F32).astype(BF)
    d_rows = (jnp.dot(pick, out_grad[...], preferred_element_type=F32) * scale).astype(BF)
    for half in range(2):
        part = slice(half * HALF, (half + 1) * HALF)
        out[:, 2 * part.start : 2 * part.start + HALF] = x_rows[:, part]
        out[:, 2 * part.start + HALF : 2 * part.start + 2 * HALF] = d_rows[:, part]


def over_rows(mask, values):
    pick = jnp.where(mask, 1.0, 0.0).astype(BF)
    return lax.dot_general(pick, values, (((0,), (0,)), ((), ())), preferred_element_type=F32)


def combine_kernel(meta, ids, gates, out_grad, result, combined, gate_part):
    used, first, second = route_masks(meta, ids)
    values = result[...]
    grad = out_grad[...].astype(F32)
    total = jnp.zeros((128, 512), F32)
    for k, mask in enumerate((used & first, used & second)):
        rows = over_rows(mask, values)
        gate = jnp.transpose(jnp.broadcast_to(gates[k : k + 1, :], (128, 128)))[:, 0:1]
        total = total + rows * gate
        part = jnp.sum(rows * grad, axis=1, keepdims=True)
        gate_part[k : k + 1, :] = jnp.transpose(jnp.broadcast_to(part, (128, 128)))[0:1, :]
    combined[...] = total.astype(BF)


def token_grad_kernel(meta, ids, result, token_grad):
    used, _, _ = route_masks(meta, ids)
    token_grad[...] = over_rows(used, result[...]).astype(BF)


def on_core(meta, c, action):
    @pl.when(meta[3] == c)
    def _():
        action()


def place(zr, xr, half):
    row, column = (xr >> 1) * PAIR, zr * 1024 + (xr & 1) * 512 + half * HALF
    return slice(row, row + PAIR), slice(column, column + HALF)


def take(refs, js):
    return {j: tuple(refs.pop(0) for _ in range(2 if j == 2 else 1)) for j in js}


def block_of(piece, i):
    each = 4 // len(piece)
    return piece[i // each].at[i % each]


def fetch_pieces(meta, own, other, target, sems, zr, xr):
    waits = []
    for half in range(2):
        rows, columns = place(zr, xr, half)
        for c in range(2):
            arrays = own if half == c else other
            source = block_of(arrays[zr], xr) if half == 0 else block_of(arrays[xr], zr)
            copy = pltpu.make_async_copy(source, target.at[rows, columns], sems.at[zr, 2 * xr + half])
            on_core(meta, c, copy.start)
        waits.append(copy)
    return waits


def column_start(meta, zr, q):
    return jnp.bitwise_xor(meta[0], zr) * 1024 + jnp.bitwise_xor(meta[1], q) * 512


def weight_part(meta, weight, kind, j, by_rows):
    parts = []
    for n in range(4 if kind else 2):
        start = column_start(meta, n, j & 1) + HALF if kind else column_start(meta, j, n)
        span = pl.ds(pl.multiple_of(start, HALF), HALF)
        parts.append(weight[span, :] if by_rows else weight[:, span])
    return jnp.concatenate(parts, axis=0 if by_rows else 1)


def times(left, right, right_by_rows):
    dims = (((1,), (0,)), ((), ())) if right_by_rows else (((1,), (1,)), ((), ()))
    return lax.dot_general(left, right, dims, preferred_element_type=F32)


def gelu_parts(pre):
    square = pre * pre
    inner = GELU_C * (pre + GELU_K * square * pre)
    tanh = jnp.tanh(inner)
    value = 0.5 * pre * (1.0 + tanh)
    slope = 0.5 * (1.0 + tanh) + 0.5 * pre * (1.0 - tanh * tanh) * GELU_C * (1.0 + 3.0 * GELU_K * square)
    return value, slope


def rows_in_kernel(js, backward, first, last, meta, weight, *refs):
    refs = list(refs)
    before = None if first else refs.pop(0)
    slope_in = refs.pop(0) if last and backward else None
    own, other = take(refs, js), take(refs, js)
    outs = refs

    def add(kind0, kind1):
        for side in range(2):
            part = slice(side * PAIR, (side + 1) * PAIR)
            total = None if first else before[part, :]
            for j in js:
                rows = jnp.concatenate([block_of(kind0[j], 2 * side + q)[...] for q in range(2)], axis=1)
                term = times(rows, weight_part(meta, weight, 0, j, not backward), not backward)
                total = term if total is None else total + term
                if j >> 1 == side:
                    rows = jnp.concatenate([block_of(kind1[j], zr)[...] for zr in range(4)], axis=1)
                    total = total + times(rows, weight_part(meta, weight, 1, j, not backward), not backward)
            if not last:
                outs[0][part, :] = total
            elif backward:
                outs[0][part, :] = (total * slope_in[part, :]).astype(BF)
            else:
                value, slope = gelu_parts(total)
                outs[0][part, :] = value.astype(BF)
                outs[1][part, :] = slope

    on_core(meta, 0, lambda: add(own, other))
    on_core(meta, 1, lambda: add(other, own))


def rows_in(js, meta, weight, own, other, before=None, slope=None, last=False, backward=False):
    first = before is None
    wide = jax.ShapeDtypeStruct((2 * PAIR, 512), F32)
    rounded = jax.ShapeDtypeStruct((2 * PAIR, 512), BF)
    outs = wide if not last else (rounded if backward else (rounded, wide))
    extra = ([] if first else [before]) + ([slope] if slope is not None else [])
    count = len(js)
    pieces = jax.tree.leaves([[v[j] for j in js] for v in (own, other)])
    return call(
        functools.partial(rows_in_kernel, js, backward, first, last),
        ("grad_hidden" if backward else "hidden") + "".join(str(j) for j in js),
        outs,
        (VMEM, VMEM) if last and not backward else VMEM,
        [SMEM] + [VMEM] * (1 + len(extra) + len(pieces)),
        [],
        count * PAIR * 4096 * 512,
        count * 4 * 1024 * 1024,
        [meta, weight] + extra + pieces,
    )


def rows_out_kernel(js, backward, adding, passing, meta, weight, source, *refs):
    refs = list(refs)
    arrived = take(refs, js) if adding else None
    passed = (refs.pop(0), refs.pop(0)) if passing else None
    outs = take(refs, js)

    def make(kind):
        for j in js:
            right = weight_part(meta, weight, kind, j, backward)
            if kind:
                part = slice((j >> 1) * PAIR, ((j >> 1) + 1) * PAIR)
                made = times(source[part, :], right, not backward)
                blocks = [made[:, zr * HALF : (zr + 1) * HALF] for zr in range(4)]
            else:
                blocks = []
                for side in range(2):
                    made = times(source[side * PAIR : (side + 1) * PAIR, :], right, not backward)
                    blocks += [made[:, :HALF], made[:, HALF:]]
            for i, block in enumerate(blocks):
                if adding:
                    block = block + block_of(arrived[j], i)[...].astype(F32)
                if passing and j == (3 if i < 2 else 1):
                    block = block + passed[i // 2][i % 2].astype(F32)
                block_of(outs[j], i)[...] = block.astype(BF)

    for c in range(2):
        on_core(meta, c, functools.partial(make, c if adding else 1 - c))


def rows_out(js, meta, weight, source, backward, arrived=None, passed=None):
    adding, passing = arrived is not None, passed is not None
    count = len(js)
    extra = (jax.tree.leaves([arrived[j] for j in js]) if adding else []) + (list(passed) if passing else [])
    shapes = [jax.ShapeDtypeStruct((2 if j == 2 else 4, PAIR, HALF), BF) for j in js for _ in range(2 if j == 2 else 1)]
    made = call(
        functools.partial(rows_out_kernel, js, backward, adding, passing),
        ("back" if backward else "out") + ("_own" if adding else "_other") + "".join(str(j) for j in js),
        tuple(shapes),
        (VMEM,) * len(shapes),
        [SMEM, VMEM, VMEM] + [VMEM] * len(extra),
        [],
        count * PAIR * 1024 * 512,
        count * 3 * 1024 * 1024,
        [meta, weight, source] + extra,
    )
    return take(list(made), js)


def weight_grad_kernel(first, meta, side, *refs):
    refs = list(refs)
    own, other = take(refs, range(4)), take(refs, range(4))
    out, rows, made, row_sems, out_sems = refs
    waits = []
    for zr in range(4):
        waits.append([])
        for xr in range(4):
            waits[zr] += fetch_pieces(meta, own, other, rows, row_sems, zr, xr)
    dims = (((0,), (0,)), ((), ()))
    leaving = []
    for zr in range(4):
        for copy in waits[zr]:
            copy.wait()
        block = rows[:, zr * 1024 : (zr + 1) * 1024]
        if first:
            term = lax.dot_general(block, side[...], dims, preferred_element_type=F32)
        else:
            term = lax.dot_general(side[...], block, dims, preferred_element_type=F32)
        made[zr] = term.astype(BF)
        for q in range(2):
            span = pl.ds(pl.multiple_of(column_start(meta, zr, q), 512), 512)
            part = slice(q * 512, (q + 1) * 512)
            source = made.at[zr, part, :] if first else made.at[zr, :, part]
            target = out.at[span, :] if first else out.at[:, span]
            copy = pltpu.make_async_copy(source, target, out_sems.at[zr, q])
            copy.start()
            leaving.append(copy)
    for copy in leaving:
        copy.wait()


def weight_grad(meta, first, side, own, other):
    return call(
        functools.partial(weight_grad_kernel, first),
        "w_in_grad" if first else "w_out_grad",
        jax.ShapeDtypeStruct((4096, 512) if first else (512, 4096), BF),
        ANY,
        [SMEM, VMEM] + [ANY] * 10,
        [
            pltpu.VMEM((2 * PAIR, 4096), BF),
            pltpu.VMEM((4, 1024, 512) if first else (4, 512, 1024), BF),
            pltpu.SemaphoreType.DMA((4, 8)),
            pltpu.SemaphoreType.DMA((4, 2)),
        ],
        2 * 2 * PAIR * 4096 * 512,
        14 * 1024 * 1024,
        [meta, side] + jax.tree.leaves([[v[j] for j in range(4)] for v in (own, other)]),
        limit=48 if first else 56,
    )


PLANE = ("xh", "c", "z", "xl")


def swap_by_core(value, stage, j):
    pairs = []
    for xh in range(2):
        for c in range(2):
            for z in range(4):
                for xl in range(2):
                    x, to_z = 2 * xh + xl, z
                    if c == stage:
                        x = x ^ j
                    else:
                        to_z = z ^ j
                    source = ((xh * 2 + c) * 4 + z) * 2 + xl
                    target = (((x >> 1) * 2 + c) * 4 + to_z) * 2 + (x & 1)
                    pairs.append((source, target))
    return lax.ppermute(value, PLANE, pairs)


def after(value, other):
    return value if other is None else lax.optimization_barrier((value, other))[0]


def to_experts(rows):
    parts = [rows[CAP * j : CAP * (j + 1)] for j in range(4)]
    return jnp.concatenate([parts[0]] + [swap(parts[j], "y", j) for j in range(1, 4)], axis=0)


def by_core(first, second, axis):
    return jnp.where(
        lax.axis_index("c") == 0,
        jnp.concatenate([first, second], axis=axis),
        jnp.concatenate([second, first], axis=axis),
    )


def first_stage(rows):
    c = lax.axis_index("c")
    mine = lax.dynamic_slice_in_dim(rows, c * 512, 512, 1)
    yours = lax.dynamic_slice_in_dim(rows, (1 - c) * 512, 512, 1)
    both = by_core(mine, swap(yours, "c", 1), 0)
    x_part, d_part = both[:, :HALF], both[:, HALF:]
    x_block = jnp.stack([x_part] + [swap_by_core(x_part, 0, j) for j in range(1, 4)])
    d_part = after(d_part, x_block)
    return x_block, jnp.stack([d_part] + [swap_by_core(d_part, 0, j) for j in range(1, 4)])


def near(block, stage):
    return {j: (swap_by_core(block, stage, j),) for j in (1, 3)}


def beyond(pieces, stage):
    return (swap_by_core(pieces[3][0][:2], stage, 1), swap_by_core(pieces[1][0][2:], stage, 3))


def through(pieces, stage):
    return (swap_by_core(pieces[2][0], stage, 1), swap_by_core(pieces[2][1], stage, 3))


def sum_first(pieces, arrived):
    arrived = [pieces[0][0], arrived[1][0], arrived[3][0]]
    return [sum(a[i].astype(F32) for a in arrived).astype(BF) for i in range(4)]


def sum_second(parts, hold=None):
    arrived = [parts[0]] + [after(swap_by_core(parts[j], 0, j), hold) for j in range(1, 4)]
    return sum(a.astype(F32) for a in arrived).astype(BF)


def to_home(both):
    c = lax.axis_index("c")
    mine = lax.dynamic_slice_in_dim(both, c * ROWS, ROWS, 0)
    yours = lax.dynamic_slice_in_dim(both, (1 - c) * ROWS, ROWS, 0)
    return by_core(mine, swap(yours, "c", 1), 1)


def across(pieces):
    return jax.tree.map(lambda v: swap(v, "c", 1), pieces)


def ordered(pieces, other):
    return {j: after(v, other) for j, v in pieces.items()}


def local(tokens, gates, expert_ids, w_in, w_out, out_grad):
    meta = jnp.stack([lax.axis_index(name) for name in ("z", "xl", "y", "c")]).astype(jnp.int32)
    ids = expert_ids.T
    gates_t = gates.T
    w_first, w_second = w_in[0], w_out[0]
    rows = call(
        select_kernel, "select", jax.ShapeDtypeStruct((ROWS, 1024), BF), VMEM, [SMEM] + [VMEM] * 4, [], 10**8, 10**6,
        [meta, ids, gates_t, tokens, out_grad], limit=60,
    )
    x_block, d_block = first_stage(to_experts(rows))

    x = {0: (x_block,), **ordered(near(x_block, 1), d_block)}
    x_other = across(x)
    pre = rows_in((0,), meta, w_first, x, x_other)
    pre = rows_in((1, 3), meta, w_first, x, x_other, pre)
    d_near = near(after(d_block, (x[1], x[3])), 1)
    x[2] = after(beyond(x, 1), pre)
    x_other[2] = across(x[2])
    hidden, slope = rows_in((2,), meta, w_first, x, x_other, pre, last=True)

    out_near = rows_out((0, 2), meta, w_second, hidden, False)
    d = {0: (d_block,), **ordered(d_near, out_near)}
    d_other = across(d)
    out_far = across(rows_out((1, 3), meta, w_second, after(hidden, out_near), False))
    grad = rows_in((0,), meta, w_second, d, d_other, backward=True)
    out = rows_out((0, 2), meta, w_second, hidden, False, ordered(across(out_near), grad))
    passed = through(out, 1)
    grad = rows_in((1, 3), meta, w_second, d, d_other, after(grad, out), backward=True)
    d[2] = after(beyond(d, 1), (out, grad))
    d_other[2] = across(d[2])
    grad_pre = rows_in((2,), meta, w_second, d, d_other, grad, slope, last=True, backward=True)
    back_near = rows_out((0, 2), meta, w_first, grad_pre, True)
    out.update(rows_out((1, 3), meta, w_second, after(hidden, back_near), False, out_far, passed))
    out_arrived = {j: (swap_by_core(out[j][0], 1, j),) for j in (1, 3)}
    back_far = across(rows_out((1, 3), meta, w_first, after(grad_pre, back_near), True))
    back = rows_out((0, 2), meta, w_first, grad_pre, True, ordered(across(back_near), out))
    passed = through(ordered(back, back_far), 1)

    w_in_grad = weight_grad(meta, True, after(grad_pre, back), x, x_other)
    out_parts = sum_first(out, ordered(out_arrived, w_in_grad))
    back.update(rows_out((1, 3), meta, w_first, grad_pre, True, back_far, after(passed, (w_in_grad, out_parts))))
    back_arrived = {j: (swap_by_core(back[j][0], 1, j),) for j in (1, 3)}
    w_out_grad = weight_grad(meta, False, after(hidden, (w_in_grad, back, out_parts)), d, d_other)
    out_sum = sum_second(out_parts, w_out_grad)
    back_parts = sum_first(back, ordered(back_arrived, w_out_grad))
    back_home = to_home(sum_second(back_parts))
    out_result = to_experts(to_home(out_sum))
    combined, gate_part = call(
        combine_kernel, "combine",
        (jax.ShapeDtypeStruct((128, 512), BF), jax.ShapeDtypeStruct((2, 128), F32)), (VMEM, VMEM),
        [SMEM] + [VMEM] * 4, [], 10**8, 10**6, [meta, ids, gates_t, out_grad, after(out_result, back_home)],
    )
    back_result = to_experts(back_home)

    gate_part = sum([swap(gate_part, "z", j) for j in range(1, 4)], gate_part)
    gate_part = gate_part + swap(gate_part, X, 1)
    token_grad = call(
        token_grad_kernel, "token_grad", jax.ShapeDtypeStruct((128, 512), BF), VMEM,
        [SMEM] + [VMEM] * 2, [], 10**8, 10**6, [meta, ids, back_result],
    )
    return combined, token_grad, gate_part.T, w_in_grad[None], w_out_grad[None]


def solution(mesh):
    fine = Mesh(mesh.devices.reshape(4, 2, 2, 4, 2), ("y", "xh", "c", "z", "xl"))
    expert, tensor = ("y", "xh", "c"), ("z", "xl")
    return jax.shard_map(
        local,
        mesh=fine,
        in_specs=(
            P(expert, tensor),
            P(expert, None),
            P(expert, None),
            P(expert, None, tensor),
            P(expert, tensor, None),
            P(expert, tensor),
        ),
        out_specs=(
            P(expert, tensor),
            P(expert, tensor),
            P(expert, None),
            P(expert, None, tensor),
            P(expert, tensor, None),
        ),
        check_vma=False,
    )
```

```python
import functools

import jax
import jax.numpy as jnp
from jax import lax
from jax.experimental import pallas as pl
from jax.experimental.pallas import tpu as pltpu
from jax.sharding import Mesh, PartitionSpec as P

CAP = 68
ROWS = 4 * CAP
PAIR = 2 * ROWS
HALF = 256
X = ("xh", "xl")

GELU_C = 0.7978845608028654
GELU_K = 0.044715
BF = jnp.bfloat16
F32 = jnp.float32
ANY = pl.BlockSpec(memory_space=pl.ANY)
SMEM = pl.BlockSpec(memory_space=pltpu.SMEM)
VMEM = pl.BlockSpec(memory_space=pltpu.VMEM)


def swap(value, axis, j):
    size = 2 if axis == "c" else 4
    return lax.ppermute(value, axis, [(i, i ^ j) for i in range(size)])


def call(kernel, name, outs, out_specs, in_specs, scratch, flops, moved, args, limit=24):
    return pl.pallas_call(
        kernel,
        name=name,
        out_shape=outs,
        in_specs=in_specs,
        out_specs=out_specs,
        scratch_shapes=scratch,
        compiler_params=pltpu.CompilerParams(vmem_limit_bytes=limit * 1024 * 1024),
        cost_estimate=pl.CostEstimate(flops=flops // 16, bytes_accessed=moved // 16, transcendentals=0),
    )(*args)


def route_masks(meta, ids):
    y = meta[2]
    rank = lax.broadcasted_iota(jnp.int32, (8, 128), 0)
    expert = jnp.bitwise_xor(rank, y)
    first = ids[0:1, :] == expert
    second = ids[1:2, :] == expert
    member = jnp.where(first | second, 1.0, 0.0).astype(F32)
    earlier = lax.broadcasted_iota(jnp.int32, (128, 128), 0) < lax.broadcasted_iota(jnp.int32, (128, 128), 1)
    slot = jnp.dot(member.astype(BF), jnp.where(earlier, 1.0, 0.0).astype(BF), preferred_element_type=F32)
    slot = jnp.where(member > 0.0, slot, -1.0)
    row = lax.broadcasted_iota(jnp.int32, (ROWS, 128), 0)
    part = (row >= CAP).astype(jnp.int32) + (row >= 2 * CAP).astype(jnp.int32) + (row >= 3 * CAP).astype(jnp.int32)
    place = (row - CAP * part).astype(F32)

    def by_part(table):
        out = jnp.broadcast_to(table[0:1, :], (ROWS, 128))
        for j in range(1, 4):
            out = jnp.where(part == j, jnp.broadcast_to(table[j : j + 1, :], (ROWS, 128)), out)
        return out

    used = by_part(slot) == place
    return used, by_part(first.astype(F32)) > 0.0, by_part(second.astype(F32)) > 0.0


def select_kernel(meta, ids, gates, tokens, out_grad, out):
    used, first, second = route_masks(meta, ids)
    pick = jnp.where(used, 1.0, 0.0).astype(BF)
    weight = jnp.where(used & first, gates[0:1, :], 0.0) + jnp.where(used & second, gates[1:2, :], 0.0)
    scale = jnp.sum(weight, axis=1, keepdims=True)
    x_rows = jnp.dot(pick, tokens[...], preferred_element_type=F32).astype(BF)
    d_rows = (jnp.dot(pick, out_grad[...], preferred_element_type=F32) * scale).astype(BF)
    for half in range(2):
        part = slice(half * HALF, (half + 1) * HALF)
        out[:, 2 * part.start : 2 * part.start + HALF] = x_rows[:, part]
        out[:, 2 * part.start + HALF : 2 * part.start + 2 * HALF] = d_rows[:, part]


def over_rows(mask, values):
    pick = jnp.where(mask, 1.0, 0.0).astype(BF)
    return lax.dot_general(pick, values, (((0,), (0,)), ((), ())), preferred_element_type=F32)


def combine_kernel(meta, ids, gates, out_grad, result, combined, gate_part):
    used, first, second = route_masks(meta, ids)
    values = result[...]
    grad = out_grad[...].astype(F32)
    total = jnp.zeros((128, 512), F32)
    for k, mask in enumerate((used & first, used & second)):
        rows = over_rows(mask, values)
        gate = jnp.transpose(jnp.broadcast_to(gates[k : k + 1, :], (128, 128)))[:, 0:1]
        total = total + rows * gate
        part = jnp.sum(rows * grad, axis=1, keepdims=True)
        gate_part[k : k + 1, :] = jnp.transpose(jnp.broadcast_to(part, (128, 128)))[0:1, :]
    combined[...] = total.astype(BF)


def token_grad_kernel(meta, ids, result, token_grad):
    used, _, _ = route_masks(meta, ids)
    token_grad[...] = over_rows(used, result[...]).astype(BF)


def on_core(meta, c, action):
    @pl.when(meta[3] == c)
    def _():
        action()


def place(zr, xr, half):
    row, column = (xr >> 1) * PAIR, zr * 1024 + (xr & 1) * 512 + half * HALF
    return slice(row, row + PAIR), slice(column, column + HALF)


def take(refs, js):
    return {j: tuple(refs.pop(0) for _ in range(2 if j == 2 else 1)) for j in js}


def block_of(piece, i):
    each = 4 // len(piece)
    return piece[i // each].at[i % each]


def fetch_pieces(meta, own, other, target, sems, zr, xr):
    waits = []
    for half in range(2):
        rows, columns = place(zr, xr, half)
        for c in range(2):
            arrays = own if half == c else other
            source = block_of(arrays[zr], xr) if half == 0 else block_of(arrays[xr], zr)
            copy = pltpu.make_async_copy(source, target.at[rows, columns], sems.at[zr, 2 * xr + half])
            on_core(meta, c, copy.start)
        waits.append(copy)
    return waits


def column_start(meta, zr, q):
    return jnp.bitwise_xor(meta[0], zr) * 1024 + jnp.bitwise_xor(meta[1], q) * 512


def weight_part(meta, weight, kind, j, by_rows):
    parts = []
    for n in range(4 if kind else 2):
        start = column_start(meta, n, j & 1) + HALF if kind else column_start(meta, j, n)
        span = pl.ds(pl.multiple_of(start, HALF), HALF)
        parts.append(weight[span, :] if by_rows else weight[:, span])
    return jnp.concatenate(parts, axis=0 if by_rows else 1)


def times(left, right, right_by_rows):
    dims = (((1,), (0,)), ((), ())) if right_by_rows else (((1,), (1,)), ((), ()))
    return lax.dot_general(left, right, dims, preferred_element_type=F32)


def gelu_parts(pre):
    square = pre * pre
    inner = GELU_C * (pre + GELU_K * square * pre)
    tanh = jnp.tanh(inner)
    value = 0.5 * pre * (1.0 + tanh)
    slope = 0.5 * (1.0 + tanh) + 0.5 * pre * (1.0 - tanh * tanh) * GELU_C * (1.0 + 3.0 * GELU_K * square)
    return value, slope


def rows_in_kernel(js, backward, first, last, meta, weight, *refs):
    refs = list(refs)
    before = None if first else refs.pop(0)
    slope_in = refs.pop(0) if last and backward else None
    own, other = take(refs, js), take(refs, js)
    outs = refs

    def add(kind0, kind1):
        for side in range(2):
            part = slice(side * PAIR, (side + 1) * PAIR)
            total = None if first else before[part, :]
            for j in js:
                rows = jnp.concatenate([block_of(kind0[j], 2 * side + q)[...] for q in range(2)], axis=1)
                term = times(rows, weight_part(meta, weight, 0, j, not backward), not backward)
                total = term if total is None else total + term
                if j >> 1 == side:
                    rows = jnp.concatenate([block_of(kind1[j], zr)[...] for zr in range(4)], axis=1)
                    total = total + times(rows, weight_part(meta, weight, 1, j, not backward), not backward)
            if not last:
                outs[0][part, :] = total
            elif backward:
                outs[0][part, :] = (total * slope_in[part, :]).astype(BF)
            else:
                value, slope = gelu_parts(total)
                outs[0][part, :] = value.astype(BF)
                outs[1][part, :] = slope

    on_core(meta, 0, lambda: add(own, other))
    on_core(meta, 1, lambda: add(other, own))


def rows_in(js, meta, weight, own, other, before=None, slope=None, last=False, backward=False):
    first = before is None
    wide = jax.ShapeDtypeStruct((2 * PAIR, 512), F32)
    rounded = jax.ShapeDtypeStruct((2 * PAIR, 512), BF)
    outs = wide if not last else (rounded if backward else (rounded, wide))
    extra = ([] if first else [before]) + ([slope] if slope is not None else [])
    count = len(js)
    pieces = jax.tree.leaves([[v[j] for j in js] for v in (own, other)])
    return call(
        functools.partial(rows_in_kernel, js, backward, first, last),
        ("grad_hidden" if backward else "hidden") + "".join(str(j) for j in js),
        outs,
        (VMEM, VMEM) if last and not backward else VMEM,
        [SMEM] + [VMEM] * (1 + len(extra) + len(pieces)),
        [],
        count * PAIR * 4096 * 512,
        count * 4 * 1024 * 1024,
        [meta, weight] + extra + pieces,
    )


def rows_out_kernel(js, backward, adding, passing, meta, weight, source, *refs):
    refs = list(refs)
    arrived = take(refs, js) if adding else None
    passed = (refs.pop(0), refs.pop(0)) if passing else None
    outs = take(refs, js)

    def make(kind):
        for j in js:
            right = weight_part(meta, weight, kind, j, backward)
            if kind:
                part = slice((j >> 1) * PAIR, ((j >> 1) + 1) * PAIR)
                made = times(source[part, :], right, not backward)
                blocks = [made[:, zr * HALF : (zr + 1) * HALF] for zr in range(4)]
            else:
                blocks = []
                for side in range(2):
                    made = times(source[side * PAIR : (side + 1) * PAIR, :], right, not backward)
                    blocks += [made[:, :HALF], made[:, HALF:]]
            for i, block in enumerate(blocks):
                if adding:
                    block = block + block_of(arrived[j], i)[...].astype(F32)
                if passing and j == (3 if i < 2 else 1):
                    block = block + passed[i // 2][i % 2].astype(F32)
                block_of(outs[j], i)[...] = block.astype(BF)

    for c in range(2):
        on_core(meta, c, functools.partial(make, c if adding else 1 - c))


def rows_out(js, meta, weight, source, backward, arrived=None, passed=None):
    adding, passing = arrived is not None, passed is not None
    count = len(js)
    extra = (jax.tree.leaves([arrived[j] for j in js]) if adding else []) + (list(passed) if passing else [])
    shapes = [jax.ShapeDtypeStruct((2 if j == 2 else 4, PAIR, HALF), BF) for j in js for _ in range(2 if j == 2 else 1)]
    made = call(
        functools.partial(rows_out_kernel, js, backward, adding, passing),
        ("back" if backward else "out") + ("_own" if adding else "_other") + "".join(str(j) for j in js),
        tuple(shapes),
        (VMEM,) * len(shapes),
        [SMEM, VMEM, VMEM] + [VMEM] * len(extra),
        [],
        count * PAIR * 1024 * 512,
        count * 3 * 1024 * 1024,
        [meta, weight, source] + extra,
    )
    return take(list(made), js)


def weight_grad_kernel(first, meta, side, *refs):
    refs = list(refs)
    own, other = take(refs, range(4)), take(refs, range(4))
    out, rows, made, row_sems, out_sems = refs
    waits = []
    for zr in range(4):
        waits.append([])
        for xr in range(4):
            waits[zr] += fetch_pieces(meta, own, other, rows, row_sems, zr, xr)
    dims = (((0,), (0,)), ((), ()))
    leaving = []
    for zr in range(4):
        for copy in waits[zr]:
            copy.wait()
        block = rows[:, zr * 1024 : (zr + 1) * 1024]
        if first:
            term = lax.dot_general(block, side[...], dims, preferred_element_type=F32)
        else:
            term = lax.dot_general(side[...], block, dims, preferred_element_type=F32)
        made[zr] = term.astype(BF)
        for q in range(2):
            span = pl.ds(pl.multiple_of(column_start(meta, zr, q), 512), 512)
            part = slice(q * 512, (q + 1) * 512)
            source = made.at[zr, part, :] if first else made.at[zr, :, part]
            target = out.at[span, :] if first else out.at[:, span]
            copy = pltpu.make_async_copy(source, target, out_sems.at[zr, q])
            copy.start()
            leaving.append(copy)
    for copy in leaving:
        copy.wait()


def weight_grad(meta, first, side, own, other):
    return call(
        functools.partial(weight_grad_kernel, first),
        "w_in_grad" if first else "w_out_grad",
        jax.ShapeDtypeStruct((4096, 512) if first else (512, 4096), BF),
        ANY,
        [SMEM, VMEM] + [ANY] * 10,
        [
            pltpu.VMEM((2 * PAIR, 4096), BF),
            pltpu.VMEM((4, 1024, 512) if first else (4, 512, 1024), BF),
            pltpu.SemaphoreType.DMA((4, 8)),
            pltpu.SemaphoreType.DMA((4, 2)),
        ],
        2 * 2 * PAIR * 4096 * 512,
        14 * 1024 * 1024,
        [meta, side] + jax.tree.leaves([[v[j] for j in range(4)] for v in (own, other)]),
        limit=48 if first else 56,
    )


PLANE = ("xh", "c", "z", "xl")


def swap_by_core(value, stage, j):
    pairs = []
    for xh in range(2):
        for c in range(2):
            for z in range(4):
                for xl in range(2):
                    x, to_z = 2 * xh + xl, z
                    if c == stage:
                        x = x ^ j
                    else:
                        to_z = z ^ j
                    source = ((xh * 2 + c) * 4 + z) * 2 + xl
                    target = (((x >> 1) * 2 + c) * 4 + to_z) * 2 + (x & 1)
                    pairs.append((source, target))
    return lax.ppermute(value, PLANE, pairs)


def after(value, other):
    return value if other is None else lax.optimization_barrier((value, other))[0]


def to_experts(rows):
    parts = [rows[CAP * j : CAP * (j + 1)] for j in range(4)]
    return jnp.concatenate([parts[0]] + [swap(parts[j], "y", j) for j in range(1, 4)], axis=0)


def by_core(first, second, axis):
    return jnp.where(
        lax.axis_index("c") == 0,
        jnp.concatenate([first, second], axis=axis),
        jnp.concatenate([second, first], axis=axis),
    )


def first_stage(rows):
    c = lax.axis_index("c")
    mine = lax.dynamic_slice_in_dim(rows, c * 512, 512, 1)
    yours = lax.dynamic_slice_in_dim(rows, (1 - c) * 512, 512, 1)
    both = by_core(mine, swap(yours, "c", 1), 0)
    x_part, d_part = both[:, :HALF], both[:, HALF:]
    x_block = jnp.stack([x_part] + [swap_by_core(x_part, 0, j) for j in range(1, 4)])
    d_part = after(d_part, x_block)
    return x_block, jnp.stack([d_part] + [swap_by_core(d_part, 0, j) for j in range(1, 4)])


def near(block, stage):
    return {j: (swap_by_core(block, stage, j),) for j in (1, 3)}


def beyond(pieces, stage):
    return (swap_by_core(pieces[3][0][:2], stage, 1), swap_by_core(pieces[1][0][2:], stage, 3))


def through(pieces, stage):
    return (swap_by_core(pieces[2][0], stage, 1), swap_by_core(pieces[2][1], stage, 3))


def sum_first(pieces, arrived):
    arrived = [pieces[0][0], arrived[1][0], arrived[3][0]]
    return [sum(a[i].astype(F32) for a in arrived).astype(BF) for i in range(4)]


def sum_second(parts, hold=None):
    arrived = [parts[0]] + [after(swap_by_core(parts[j], 0, j), hold) for j in range(1, 4)]
    return sum(a.astype(F32) for a in arrived).astype(BF)


def to_home(both):
    c = lax.axis_index("c")
    mine = lax.dynamic_slice_in_dim(both, c * ROWS, ROWS, 0)
    yours = lax.dynamic_slice_in_dim(both, (1 - c) * ROWS, ROWS, 0)
    return by_core(mine, swap(yours, "c", 1), 1)


def across(pieces):
    return jax.tree.map(lambda v: swap(v, "c", 1), pieces)


def ordered(pieces, other):
    return {j: after(v, other) for j, v in pieces.items()}


def local(tokens, gates, expert_ids, w_in, w_out, out_grad):
    meta = jnp.stack([lax.axis_index(name) for name in ("z", "xl", "y", "c")]).astype(jnp.int32)
    ids = expert_ids.T
    gates_t = gates.T
    w_first, w_second = w_in[0], w_out[0]
    rows = call(
        select_kernel, "select", jax.ShapeDtypeStruct((ROWS, 1024), BF), VMEM, [SMEM] + [VMEM] * 4, [], 10**8, 10**6,
        [meta, ids, gates_t, tokens, out_grad], limit=60,
    )
    x_block, d_block = first_stage(to_experts(rows))

    x = {0: (x_block,), **ordered(near(x_block, 1), d_block)}
    x_other = across(x)
    pre = rows_in((0,), meta, w_first, x, x_other)
    pre = rows_in((1, 3), meta, w_first, x, x_other, pre)
    d_near = near(after(d_block, (x[1], x[3])), 1)
    x[2] = after(beyond(x, 1), pre)
    x_other[2] = across(x[2])
    hidden, slope = rows_in((2,), meta, w_first, x, x_other, pre, last=True)

    out_near = rows_out((0, 2), meta, w_second, hidden, False)
    d = {0: (d_block,), **ordered(d_near, out_near)}
    d_other = across(d)
    out_far = across(rows_out((1, 3), meta, w_second, after(hidden, out_near), False))
    grad = rows_in((0,), meta, w_second, d, d_other, backward=True)
    out = rows_out((0, 2), meta, w_second, hidden, False, ordered(across(out_near), grad))
    passed = through(out, 1)
    grad = rows_in((1, 3), meta, w_second, d, d_other, after(grad, out), backward=True)
    d[2] = after(beyond(d, 1), (out, grad))
    d_other[2] = across(d[2])
    grad_pre = rows_in((2,), meta, w_second, d, d_other, grad, slope, last=True, backward=True)
    back_near = rows_out((0, 2), meta, w_first, grad_pre, True)
    out.update(rows_out((1, 3), meta, w_second, after(hidden, back_near), False, out_far, passed))
    out_arrived = {j: (swap_by_core(out[j][0], 1, j),) for j in (1, 3)}
    back_far = across(rows_out((1, 3), meta, w_first, after(grad_pre, back_near), True))
    back = rows_out((0, 2), meta, w_first, grad_pre, True, ordered(across(back_near), out))
    passed = through(ordered(back, back_far), 1)

    w_in_grad = weight_grad(meta, True, after(grad_pre, back), x, x_other)
    out_parts = sum_first(out, ordered(out_arrived, w_in_grad))
    back.update(rows_out((1, 3), meta, w_first, grad_pre, True, back_far, after(passed, (w_in_grad, out_parts))))
    back_arrived = {j: (swap_by_core(back[j][0], 1, j),) for j in (1, 3)}
    w_out_grad = weight_grad(meta, False, after(hidden, (w_in_grad, back, out_parts)), d, d_other)
    out_sum = sum_second(out_parts, w_out_grad)
    back_parts = sum_first(back, ordered(back_arrived, w_out_grad))
    back_home = to_home(sum_second(back_parts))
    out_result = to_experts(to_home(out_sum))
    combined, gate_part = call(
        combine_kernel, "combine",
        (jax.ShapeDtypeStruct((128, 512), BF), jax.ShapeDtypeStruct((2, 128), F32)), (VMEM, VMEM),
        [SMEM] + [VMEM] * 4, [], 10**8, 10**6, [meta, ids, gates_t, out_grad, after(out_result, back_home)],
    )
    back_result = to_experts(back_home)

    gate_part = sum([swap(gate_part, "z", j) for j in range(1, 4)], gate_part)
    gate_part = after(gate_part, back_result)
    gate_part = gate_part + swap(gate_part, X, 1)
    token_grad = call(
        token_grad_kernel, "token_grad", jax.ShapeDtypeStruct((128, 512), BF), VMEM,
        [SMEM] + [VMEM] * 2, [], 10**8, 10**6, [meta, ids, back_result],
    )
    return combined, token_grad, gate_part.T, w_in_grad[None], w_out_grad[None]


def solution(mesh):
    fine = Mesh(mesh.devices.reshape(4, 2, 2, 4, 2), ("y", "xh", "c", "z", "xl"))
    expert, tensor = ("y", "xh", "c"), ("z", "xl")
    return jax.shard_map(
        local,
        mesh=fine,
        in_specs=(
            P(expert, tensor),
            P(expert, None),
            P(expert, None),
            P(expert, None, tensor),
            P(expert, tensor, None),
            P(expert, tensor),
        ),
        out_specs=(
            P(expert, tensor),
            P(expert, tensor),
            P(expert, None),
            P(expert, None, tensor),
            P(expert, tensor, None),
        ),
        check_vma=False,
    )
```
